256 devices in a mesh: dom: 64 (over y_hi, x, z), lon: 4 (over y_lo, core).
Axes of the slice: x: 4, y: 4 (y_hi: 2, y_lo: 2; y = y_hi * 2 + y_lo), z: 8, core: 2. Of those that a mesh axis runs over, the one named last changes fastest.
Arguments:
- state: float32 [64, 4, 4, 128, 512], P('dom', None, None, None, 'lon'), may hold values from -6 to 6
- level_thickness: float32 [4, 128, 512], P(None, None, 'lon'), may hold values from 0.2 to 1
- wet_levels: int32 [128, 512], P(None, 'lon'), may hold values from 0 to 4
- ancestors: int32 [64, 8, 1], P('dom', 'lon'), may hold values from 0 to 63
Outputs:
- forecast: float32 [64, 4, 4, 128, 512], P('dom', None, None, None, 'lon')
The draws below stay inside these ranges and needn't reach their ends.
All inputs are finite; a program needn't handle non-finite values.
Results may differ from the reference program's by a relative error of at most 0.0003.
Values sent between devices are 32-bit elements; how exact they have to be, the bound alone decides.
No kernel may reach another device: no remote copies, remote signals or barrier semaphores. Data moves between devices by JAX's collectives and lax.ppermute only.
A program may use at most 64 MiB of HBM per device.

```python
import math
import jax
import jax.numpy as jnp
from jax import lax

LEV = 4
FIELDS = 4
TILE = 64
BLEND = 8
STEPS = 3
LAT = 128
PARTICLES = 64
LON = 512
TILES = 8


def set_ends(values, key, low, high):
    shape = values.shape
    spot = [jax.random.randint(jax.random.fold_in(key, axis), (), 0, shape[axis]) for axis in range(len(shape))]
    values = values.at[tuple(spot)].set(low)
    longest = shape.index(max(shape))
    spot[longest] = (spot[longest] + 1) % shape[longest]
    return values.at[tuple(spot)].set(high)


def block_scale(key, shape, pieces, least, high):
    level = 1.0
    for axis_at, blocks in pieces:
        draws = jax.random.uniform(jax.random.fold_in(jax.random.fold_in(key, 6), axis_at), (blocks,), jnp.float32, least / len(pieces), high / len(pieces))
        level = level * jnp.repeat(jnp.exp(draws), shape[axis_at] // blocks).reshape((-1,) + (1,) * (len(shape) - 1 - axis_at))
    return level


def different_ones(stream_key, rows, amount, top, lift):
    ranking = jax.random.permutation(jax.random.fold_in(stream_key, 1), amount)
    boost = ranking
    for power in range(3):
        boost = boost * boost // amount
    boost = boost * lift // amount
    chance = jax.random.randint(jax.random.fold_in(stream_key, 2), (rows, amount), 0, 4096) + boost
    sure = jax.random.permutation(jax.random.fold_in(stream_key, 3), rows)[jnp.arange(amount) % rows]
    chance = jnp.where(jnp.arange(rows)[:, None] == sure[None, :], 1 << 14, chance)
    score = chance * amount + jnp.arange(amount)
    return lax.top_k(score.astype(jnp.int32), top)[1].astype(jnp.int32)


def gaussian(own_key, shape, deviation, most, split=(), held_as=jnp.bfloat16):
    gain = block_scale(own_key, shape, split, -0.22, 0.18) if split else 1.0
    entries = jax.random.normal(own_key, shape, jnp.float32) * deviation * gain
    return jnp.minimum(jnp.maximum(entries, -most), most).astype(held_as)


def setup_inputs(seed: int = 0) -> dict:
    splits = jax.random.split(jax.random.key(seed), 5)
    return {
        "state": gaussian(splits[0], (PARTICLES, FIELDS, LEV, LAT, LON), 1.0, 6.0, ((0, 64), (4, 4)), jnp.float32),
        "level_thickness": jnp.clip(jnp.exp(math.log(1.0) - 1.609438 * jax.random.uniform(splits[1], (LEV, LAT, LON), jnp.float32) ** block_scale(splits[1], (LEV, LAT, LON), ((2, 4),), -0.2, 0.2)), 0.2, 1.0),
        "wet_levels": set_ends(jax.random.randint(splits[2], (LAT, LON), 0, LEV + 1), jax.random.fold_in(splits[2], 1), 0, LEV).astype(jnp.int32),
        "ancestors": different_ones(splits[3], PARTICLES * TILES, PARTICLES, 1, 256).reshape((PARTICLES, TILES, 1)),
    }


time_step = 0.3
gravity = 1.0
drag_rate = 0.05
diffusion = 0.1
vertical_mix = 0.2
coriolis_base = 0.1
coriolis_slope = 0.3


def trim_cols(array, width):
    return array[..., width:array.shape[-1] - width]


def pad_rows(array):
    return jnp.pad(array, [(0, 0)] * (array.ndim - 2) + [(1, 1), (0, 0)])


def diff_lon(array):
    return 0.5 * (array[..., 2:] - array[..., :-2])


def diff_lat(array):
    padded = pad_rows(array)
    return 0.5 * (padded[..., 2:, :] - padded[..., :-2, :])


def laplace(array):
    padded = pad_rows(array)
    centre = array[..., 1:-1]
    return array[..., 2:] + array[..., :-2] + padded[..., 2:, 1:-1] + padded[..., :-2, 1:-1] - 4.0 * centre


def advance(fields, thickness, coriolis):
    height = fields[0]
    zonal = fields[1]
    meridional = fields[2]
    tracer = fields[3]
    wetness = (thickness > 0).astype(fields.dtype)
    wet_one = trim_cols(wetness, 1)
    zonal_one = wet_one * (trim_cols(zonal, 1) + time_step * (coriolis * trim_cols(meridional, 1) - gravity * diff_lon(height) - drag_rate * trim_cols(zonal, 1)))
    merid_one = wet_one * (trim_cols(meridional, 1) + time_step * (-coriolis * trim_cols(zonal, 1) - gravity * trim_cols(diff_lat(height), 1) - drag_rate * trim_cols(meridional, 1)))
    depth_one = trim_cols(thickness, 1)
    wet_two = trim_cols(wetness, 2)
    height_two = wet_two * (trim_cols(height, 2) - time_step * (diff_lon(depth_one * zonal_one) + trim_cols(diff_lat(depth_one * merid_one), 1)))
    tracer_one = trim_cols(tracer, 1)
    transport = diff_lon(zonal_one * tracer_one) + trim_cols(diff_lat(merid_one * tracer_one), 1)
    tracer_two = wet_two * (trim_cols(tracer, 2) - time_step * transport + diffusion * trim_cols(laplace(tracer), 1))
    exchanged = vertical_mix * wet_two[1:] * wet_two[:-1] * (tracer_two[1:] - tracer_two[:-1])
    zero_layer = jnp.zeros_like(tracer_two[:1])
    tracer_two = tracer_two + jnp.concatenate([exchanged, zero_layer], 0) - jnp.concatenate([zero_layer, exchanged], 0)
    return jnp.stack([height_two, trim_cols(zonal_one, 1), trim_cols(merid_one, 1), tracer_two])


def edge_weight(position):
    near_left = position < BLEND
    near_right = position >= TILE - BLEND
    distance = jnp.where(near_left, position, TILE - 1 - position).astype(jnp.float32)
    return jnp.where(near_left | near_right, 0.5 + (distance + 0.5) / (2.0 * BLEND), 1.0).astype(jnp.float32)


def wrap_cols(array, width):
    return jnp.concatenate([array[..., -width:], array, array[..., :width]], -1)


def reference(state, level_thickness, wet_levels, ancestors):
    lineage = ancestors[:, :, 0]
    own = jnp.repeat(lineage, TILE, axis=1)
    left = jnp.repeat(jnp.roll(lineage, 1, axis=1), TILE, axis=1)
    right = jnp.repeat(jnp.roll(lineage, -1, axis=1), TILE, axis=1)
    position = jnp.arange(LON) % TILE
    neighbour = jnp.where(position < BLEND, left, jnp.where(position >= TILE - BLEND, right, own))
    weight = edge_weight(position)
    columns = jnp.arange(LON)
    mask = (jnp.arange(LEV)[:, None, None] < wet_levels[None]).astype(state.dtype)
    thickness = level_thickness * mask
    thick_pad = wrap_cols(thickness, 2)
    coriolis = (coriolis_base + coriolis_slope * jnp.arange(LAT) / LAT)[:, None].astype(state.dtype)

    def member(indices):
        own_row, other_row = indices
        picked = jnp.moveaxis(state[own_row, :, :, :, columns], 0, -1)
        other = jnp.moveaxis(state[other_row, :, :, :, columns], 0, -1)
        fields = weight * picked + (1.0 - weight) * other
        for substep in range(STEPS):
            fields = advance(wrap_cols(fields, 2), thick_pad, coriolis)
        return fields

    return lax.map(member, (own, neighbour))
```

```python
import jax
import jax.numpy as jnp
from jax import lax
from jax.experimental import pallas as pl
from jax.experimental.pallas import tpu as pltpu
from jax.sharding import PartitionSpec as P

LEV = 4
FIELDS = 4
TILE = 64
BLEND = 8
STEPS = 3
LAT = 128
WIDTH = 128
HALO = 2 * STEPS
GROUPS = FIELDS * LEV + LEV
PAD = 8
ROWS = 32

time_step = 0.3
gravity = 1.0
drag_rate = 0.05
diffusion = 0.1
vertical_mix = 0.2
coriolis_base = 0.1
coriolis_slope = 0.3

VMEM_LIMIT = 16 * 1024 * 1024


def lanes_of(rows):
    return lax.broadcasted_iota(jnp.int32, (rows, WIDTH), 1)


def vmem(count):
    return [pl.BlockSpec(memory_space=pltpu.VMEM)] * count


def blend_kernel(table_ref, block_ref, out_ref):
    particles, rows, _ = block_ref.shape
    lane = lanes_of(8)
    position = lane % TILE
    near_left = position < BLEND
    near_right = position >= TILE - BLEND
    distance = jnp.where(near_left, position, TILE - 1 - position).astype(jnp.float32)
    weight = jnp.where(near_left | near_right, 0.5 + (distance + 0.5) / (2.0 * BLEND), 1.0)
    rest = 1.0 - weight
    first = lane < TILE
    zero = jnp.zeros_like(weight)
    weights = (
        jnp.where(first & near_left, rest, zero),
        jnp.where(first, weight, jnp.where(near_left, rest, zero)),
        jnp.where(first, jnp.where(near_right, rest, zero), weight),
        jnp.where(first, zero, jnp.where(near_right, rest, zero)),
    )

    def one(particle, carry):
        picks = [table_ref[tile, particle] for tile in range(4)]
        for row in range(0, rows, 8):
            parts = [block_ref[pick, row : row + 8, :] * w for pick, w in zip(picks, weights)]
            out_ref[particle, row : row + 8, :] = (parts[1] + parts[2]) + (parts[0] + parts[3])
        return carry

    lax.fori_loop(0, particles, one, 0, unroll=4)


def blend(table, block):
    return pl.pallas_call(
        blend_kernel,
        out_shape=jax.ShapeDtypeStruct(block.shape, block.dtype),
        in_specs=[pl.BlockSpec(memory_space=pltpu.SMEM)] + vmem(1),
        out_specs=pl.BlockSpec(memory_space=pltpu.VMEM),
        compiler_params=pltpu.CompilerParams(vmem_limit_bytes=VMEM_LIMIT),
        cost_estimate=pl.CostEstimate(flops=4 * block.size, bytes_accessed=8 * block.size, transcendentals=0),
        name="blend",
    )(table, block)


def masked_thickness(depth_ref, levels_ref, level, start, rows):
    wet = levels_ref[pl.ds(start, rows), :] > level
    return jnp.where(wet, depth_ref[level, pl.ds(start, rows), :], 0.0)


def pack_kernel(fields_ref, depth_ref, levels_ref, right_ref, left_ref):
    lane = lanes_of(8)
    slot_right = lane // HALO
    slot_left = ((lane + WIDTH - HALO) % WIDTH) // HALO

    def one(block, carry):
        start = pl.multiple_of(block * 8, 8)
        right = jnp.zeros((8, WIDTH), jnp.float32)
        left = jnp.zeros((8, WIDTH), jnp.float32)
        for group in range(GROUPS):
            if group < FIELDS * LEV:
                values = fields_ref[group, pl.ds(start, 8), :]
            else:
                values = masked_thickness(depth_ref, levels_ref, group - FIELDS * LEV, start, 8)
            turned = pltpu.roll(values, (HALO * group + HALO) % WIDTH, 1)
            right = jnp.where(slot_right == group, turned, right)
            left = jnp.where(slot_left == group, turned, left)
        right_ref[pl.ds(start, 8), :] = right
        left_ref[pl.ds(start, 8), :] = left
        return carry

    lax.fori_loop(0, LAT // 8, one, 0, unroll=4)


def pack(fields, depth, levels):
    shape = jax.ShapeDtypeStruct((LAT, WIDTH), jnp.float32)
    return pl.pallas_call(
        pack_kernel,
        out_shape=(shape, shape),
        in_specs=vmem(3),
        out_specs=tuple(vmem(2)),
        compiler_params=pltpu.CompilerParams(vmem_limit_bytes=VMEM_LIMIT),
        cost_estimate=pl.CostEstimate(flops=4 * fields.size, bytes_accessed=5 * fields.size, transcendentals=0),
        name="pack",
    )(fields, depth, levels)


def forecast_kernel(
    fields_ref, depth_ref, levels_ref, before_ref, after_ref, out_ref,
    height, zonal, merid, tracer, thick, height_part, flux, south, north,
):
    lane = lanes_of(ROWS)
    at_first = lane == 0
    at_last = lane == WIDTH - 1

    def east(pair):
        main, rim = (pltpu.roll(x, WIDTH - 1, 1) for x in pair)
        return jnp.where(at_last, rim, main), jnp.where(at_last, main, rim)

    def west(pair):
        main, rim = (pltpu.roll(x, 1, 1) for x in pair)
        return jnp.where(at_first, rim, main), jnp.where(at_first, main, rim)

    def slope(pair):
        return tuple(e - w for e, w in zip(east(pair), west(pair)))

    def rows_at(ref, side, level, start, shift):
        return ref[side, level, pl.ds(start + PAD + shift, ROWS), :]

    def blocks(body):
        def one(block, carry):
            body(pl.multiple_of(block * ROWS, ROWS))
            return carry

        lax.fori_loop(0, LAT // ROWS, one, 0)

    def put(ref, side, level, start, values):
        ref[side, level, pl.ds(pl.multiple_of(start + PAD, 8), ROWS), :] = values

    edge = jnp.zeros((PAD, WIDTH), jnp.float32)
    for ref in (height, flux, south, north):
        for side in range(2):
            for level in range(LEV):
                ref[side, level, 0:PAD, :] = edge
                ref[side, level, PAD + LAT : 2 * PAD + LAT, :] = edge

    sources = (height, zonal, merid, tracer)
    from_before = (lane // HALO) % 2 == 0

    def load(start):
        before = before_ref[pl.ds(start, ROWS), :]
        after = after_ref[pl.ds(start, ROWS), :]
        even = jnp.where(from_before, before, after)
        odd = jnp.where(from_before, after, before)
        for group in range(GROUPS):
            rim = pltpu.roll((even, odd)[group % 2], (2 * WIDTH - HALO - HALO * group) % WIDTH, 1)
            field, level = divmod(group, LEV)
            if field < FIELDS:
                put(sources[field], 0, level, start, fields_ref[group, pl.ds(start, ROWS), :])
                put(sources[field], 1, level, start, rim)
            else:
                put(thick, 0, level, start, masked_thickness(depth_ref, levels_ref, level, start, ROWS))
                put(thick, 1, level, start, rim)

    blocks(load)

    half = 0.5 * time_step
    keep = 1.0 - time_step * drag_rate

    for step in range(STEPS):
        last = step == STEPS - 1

        def winds(start):
            row = lax.broadcasted_iota(jnp.int32, (ROWS, WIDTH), 0) + start
            turn = time_step * (coriolis_base + coriolis_slope * row.astype(jnp.float32) / LAT)
            for level in range(LEV):
                h, u, v, c, t = (
                    [rows_at(ref, side, level, start, 0) for side in range(2)]
                    for ref in (height, zonal, merid, tracer, thick)
                )
                dh = slope(h)
                new_u, new_v, across, down, up = [], [], [], [], []
                for side in range(2):
                    dy = rows_at(height, side, level, start, 1) - rows_at(height, side, level, start, -1)
                    wet = t[side] > 0.0
                    one_u = keep * u[side] + turn * v[side] - (half * gravity) * dh[side]
                    one_v = keep * v[side] - turn * u[side] - (half * gravity) * dy
                    one_u = jnp.where(wet, one_u, 0.0)
                    one_v = jnp.where(wet, one_v, 0.0)
                    some, more = diffusion * c[side], half * c[side]
                    along, cross = more * one_u, more * one_v
                    new_u.append(one_u)
                    new_v.append(one_v)
                    across.append(t[side] * one_u)
                    down.append(some - along)
                    up.append(some + along)
                    put(flux, side, level, start, t[side] * one_v)
                    put(south, side, level, start, some - cross)
                    put(north, side, level, start, some + cross)
                du = slope(across)
                from_east, from_west = east(down), west(up)
                for side in range(2):
                    if last and side:
                        continue
                    if last:
                        out_ref[LEV + level, pl.ds(start, ROWS), :] = new_u[0]
                        out_ref[2 * LEV + level, pl.ds(start, ROWS), :] = new_v[0]
                    else:
                        put(zonal, side, level, start, new_u[side])
                        put(merid, side, level, start, new_v[side])
                    put(height_part, side, level, start, h[side] - half * du[side])
                    put(
                        tracer, side, level, start,
                        (1.0 - 4.0 * diffusion) * c[side] + (from_east[side] + from_west[side]),
                    )

        def levels(start):
            for side in range(1 if last else 2):
                wets = [rows_at(thick, side, level, start, 0) > 0.0 for level in range(LEV)]
                moved = []
                for level in range(LEV):
                    dy = rows_at(flux, side, level, start, 1) - rows_at(flux, side, level, start, -1)
                    new_h = rows_at(height_part, side, level, start, 0) - half * dy
                    new_h = jnp.where(wets[level], new_h, 0.0)
                    if last:
                        out_ref[level, pl.ds(start, ROWS), :] = new_h
                    else:
                        put(height, side, level, start, new_h)
                    new_c = rows_at(tracer, side, level, start, 0) + (
                        rows_at(south, side, level, start, 1) + rows_at(north, side, level, start, -1)
                    )
                    moved.append(jnp.where(wets[level], new_c, 0.0))
                swaps = [
                    jnp.where(wets[level] & wets[level + 1], vertical_mix * (moved[level + 1] - moved[level]), 0.0)
                    for level in range(LEV - 1)
                ]
                for level in range(LEV):
                    new_c = moved[level]
                    if level < LEV - 1:
                        new_c = new_c + swaps[level]
                    if level > 0:
                        new_c = new_c - swaps[level - 1]
                    if last:
                        out_ref[3 * LEV + level, pl.ds(start, ROWS), :] = new_c
                    else:
                        put(tracer, side, level, start, new_c)

        blocks(winds)
        blocks(levels)


def run_forecast(fields, depth, levels, before, after):
    scratch = pltpu.VMEM((2, LEV, LAT + 2 * PAD, WIDTH), jnp.float32)
    return pl.pallas_call(
        forecast_kernel,
        out_shape=jax.ShapeDtypeStruct(fields.shape, fields.dtype),
        in_specs=vmem(5),
        out_specs=pl.BlockSpec(memory_space=pltpu.VMEM),
        scratch_shapes=[scratch] * 9,
        compiler_params=pltpu.CompilerParams(vmem_limit_bytes=VMEM_LIMIT),
        cost_estimate=pl.CostEstimate(flops=150 * fields.size, bytes_accessed=12 * fields.size, transcendentals=0),
        name="forecast",
    )(fields, depth, levels, before, after)


def ring(values, axis, shift):
    size = lax.axis_size(axis)
    return lax.ppermute(values, axis, [(i, (i + shift) % size) for i in range(size)])


def tile_table(ancestors):
    own = ancestors[0, :, 0]
    left = ring(own[1:], "lon", 1)
    right = ring(own[:1], "lon", -1)
    mine = jnp.concatenate([left, own, right])
    size = lax.axis_size("dom")
    here = jnp.arange(size) == lax.axis_index("dom")
    table = jnp.where(here[None, :], mine[:, None], 0)
    bit = 1
    while bit < size:
        table = table + lax.ppermute(table, "dom", [(i, i ^ bit) for i in range(size)])
        bit *= 2
    return table


def on_device(state, level_thickness, wet_levels, ancestors):
    size = lax.axis_size("dom")
    table = tile_table(ancestors)
    chunks = state.reshape(size, -1, WIDTH)
    block = lax.all_to_all(chunks, "dom", split_axis=0, concat_axis=0, tiled=True)
    mixed = blend(table, block)
    back = lax.all_to_all(mixed, "dom", split_axis=0, concat_axis=0, tiled=True)
    fields = back.reshape(FIELDS * LEV, LAT, WIDTH)
    right, left = pack(fields, level_thickness, wet_levels)
    before = ring(right, "lon", 1)
    after = ring(left, "lon", -1)
    result = run_forecast(fields, level_thickness, wet_levels, before, after)
    return result.reshape(state.shape)


def solution(mesh):
    return jax.shard_map(
        on_device,
        mesh=mesh,
        in_specs=(
            P("dom", None, None, None, "lon"),
            P(None, None, "lon"),
            P(None, "lon"),
            P("dom", "lon", None),
        ),
        out_specs=P("dom", None, None, None, "lon"),
        check_vma=False,
    )
```

```python
import jax
import jax.numpy as jnp
from jax import lax
from jax.experimental import pallas as pl
from jax.experimental.pallas import tpu as pltpu
from jax.sharding import PartitionSpec as P

LEV = 4
FIELDS = 4
TILE = 64
BLEND = 8
STEPS = 3
LAT = 128
WIDTH = 128
HALO = 2 * STEPS
GROUPS = FIELDS * LEV + LEV
PAD = 8
ROWS = 128

time_step = 0.3
gravity = 1.0
drag_rate = 0.05
diffusion = 0.1
vertical_mix = 0.2
coriolis_base = 0.1
coriolis_slope = 0.3

VMEM_LIMIT = 16 * 1024 * 1024


def lanes_of(rows):
    return lax.broadcasted_iota(jnp.int32, (rows, WIDTH), 1)


def vmem(count):
    return [pl.BlockSpec(memory_space=pltpu.VMEM)] * count


def chunk_kernel(state_ref, own_ref, left_ref, right_ref, out_ref):
    height = state_ref.shape[1]
    lane = lanes_of(1)
    picks = (left_ref[1], own_ref[0], own_ref[1], right_ref[0])
    row = jnp.zeros((1, WIDTH), jnp.int32)
    for tile, pick in enumerate(picks):
        row = jnp.where(lane == tile, pick, row)
    row = row.astype(jnp.float32)
    for chunk in range(state_ref.shape[0]):
        base = chunk * (height + 1)
        out_ref[base : base + height, :] = state_ref[chunk]
        out_ref[base + height : base + height + 1, :] = row


def make_chunks(chunks, own, left, right):
    count, height, width = chunks.shape
    shape = (count * (height + 1), width)
    return pl.pallas_call(
        chunk_kernel,
        out_shape=jax.ShapeDtypeStruct(shape, chunks.dtype),
        in_specs=vmem(1) + [pl.BlockSpec(memory_space=pltpu.SMEM)] * 3,
        out_specs=pl.BlockSpec(memory_space=pltpu.VMEM),
        compiler_params=pltpu.CompilerParams(vmem_limit_bytes=VMEM_LIMIT),
        cost_estimate=pl.CostEstimate(flops=0, bytes_accessed=8 * chunks.size, transcendentals=0),
        name="chunks",
    )(chunks, own, left, right)


def blend_kernel(block_ref, out_ref, numbers_ref, table_ref, sem):
    particles, rows, _ = out_ref.shape
    numbers_ref[...] = block_ref[pl.ds(rows, particles, stride=rows + 1), :].astype(jnp.int32)
    copy = pltpu.make_async_copy(numbers_ref, table_ref, sem)
    copy.start()
    lane = lanes_of(8)
    position = lane % TILE
    near_left = position < BLEND
    near_right = position >= TILE - BLEND
    distance = jnp.where(near_left, position, TILE - 1 - position).astype(jnp.float32)
    weight = jnp.where(near_left | near_right, 0.5 + (distance + 0.5) / (2.0 * BLEND), 1.0)
    rest = 1.0 - weight
    first = lane < TILE
    zero = jnp.zeros_like(weight)
    weights = (
        jnp.where(first & near_left, rest, zero),
        jnp.where(first, weight, jnp.where(near_left, rest, zero)),
        jnp.where(first, jnp.where(near_right, rest, zero), weight),
        jnp.where(first, zero, jnp.where(near_right, rest, zero)),
    )
    copy.wait()

    def one(particle, carry):
        picks = [table_ref[particle, tile] * (rows + 1) for tile in range(4)]
        for row in range(0, rows, 8):
            parts = [block_ref[pl.ds(pick + row, 8), :] * w for pick, w in zip(picks, weights)]
            out_ref[particle, row : row + 8, :] = (parts[1] + parts[2]) + (parts[0] + parts[3])
        return carry

    lax.fori_loop(0, particles, one, 0, unroll=4)


def blend(block, particles):
    rows = block.shape[0] // particles - 1
    shape = (particles, rows, WIDTH)
    return pl.pallas_call(
        blend_kernel,
        out_shape=jax.ShapeDtypeStruct(shape, block.dtype),
        in_specs=vmem(1),
        out_specs=pl.BlockSpec(memory_space=pltpu.VMEM),
        scratch_shapes=[
            pltpu.VMEM((particles, WIDTH), jnp.int32),
            pltpu.SMEM((particles, WIDTH), jnp.int32),
            pltpu.SemaphoreType.DMA,
        ],
        compiler_params=pltpu.CompilerParams(vmem_limit_bytes=VMEM_LIMIT),
        cost_estimate=pl.CostEstimate(flops=4 * block.size, bytes_accessed=8 * block.size, transcendentals=0),
        name="blend",
    )(block)


def masked_thickness(depth_ref, levels_ref, level, start, rows):
    wet = levels_ref[pl.ds(start, rows), :] > level
    return jnp.where(wet, depth_ref[level, pl.ds(start, rows), :], 0.0)


def pack_kernel(fields_ref, depth_ref, levels_ref, right_ref, left_ref):
    lane = lanes_of(8)
    slot_right = lane // HALO
    slot_left = ((lane + WIDTH - HALO) % WIDTH) // HALO

    def one(block, carry):
        start = pl.multiple_of(block * 8, 8)
        right = jnp.zeros((8, WIDTH), jnp.float32)
        left = jnp.zeros((8, WIDTH), jnp.float32)
        for group in range(GROUPS):
            if group < FIELDS * LEV:
                values = fields_ref[group, pl.ds(start, 8), :]
            else:
                values = masked_thickness(depth_ref, levels_ref, group - FIELDS * LEV, start, 8)
            turned = pltpu.roll(values, (HALO * group + HALO) % WIDTH, 1)
            right = jnp.where(slot_right == group, turned, right)
            left = jnp.where(slot_left == group, turned, left)
        right_ref[pl.ds(start, 8), :] = right
        left_ref[pl.ds(start, 8), :] = left
        return carry

    lax.fori_loop(0, LAT // 8, one, 0, unroll=4)


def pack(fields, depth, levels):
    shape = jax.ShapeDtypeStruct((LAT, WIDTH), jnp.float32)
    return pl.pallas_call(
        pack_kernel,
        out_shape=(shape, shape),
        in_specs=vmem(3),
        out_specs=tuple(vmem(2)),
        compiler_params=pltpu.CompilerParams(vmem_limit_bytes=VMEM_LIMIT),
        cost_estimate=pl.CostEstimate(flops=4 * fields.size, bytes_accessed=5 * fields.size, transcendentals=0),
        name="pack",
    )(fields, depth, levels)


def forecast_kernel(
    fields_ref, depth_ref, levels_ref, before_ref, after_ref, out_ref,
    height, zonal, merid, tracer, thick, height_part, flux, south, north,
):
    lane = lanes_of(ROWS)
    at_first = lane == 0
    at_last = lane == WIDTH - 1

    def east(pair):
        main, rim = (pltpu.roll(x, WIDTH - 1, 1) for x in pair)
        return jnp.where(at_last, rim, main), jnp.where(at_last, main, rim)

    def west(pair):
        main, rim = (pltpu.roll(x, 1, 1) for x in pair)
        return jnp.where(at_first, rim, main), jnp.where(at_first, main, rim)

    def slope(pair):
        return tuple(e - w for e, w in zip(east(pair), west(pair)))

    def rows_at(ref, side, level, start, shift):
        return ref[side, level, pl.ds(start + PAD + shift, ROWS), :]

    def blocks(body):
        for block in range(LAT // ROWS):
            body(block * ROWS)

    def put(ref, side, level, start, values):
        ref[side, level, pl.ds(start + PAD, ROWS), :] = values

    edge = jnp.zeros((PAD, WIDTH), jnp.float32)
    for ref in (height, flux, south, north):
        for side in range(2):
            for level in range(LEV):
                ref[side, level, 0:PAD, :] = edge
                ref[side, level, PAD + LAT : 2 * PAD + LAT, :] = edge

    sources = (height, zonal, merid, tracer)
    from_before = (lane // HALO) % 2 == 0

    def load(start):
        before = before_ref[pl.ds(start, ROWS), :]
        after = after_ref[pl.ds(start, ROWS), :]
        even = jnp.where(from_before, before, after)
        odd = jnp.where(from_before, after, before)
        for group in range(GROUPS):
            rim = pltpu.roll((even, odd)[group % 2], (2 * WIDTH - HALO - HALO * group) % WIDTH, 1)
            field, level = divmod(group, LEV)
            if field < FIELDS:
                put(sources[field], 0, level, start, fields_ref[group, pl.ds(start, ROWS), :])
                put(sources[field], 1, level, start, rim)
            else:
                put(thick, 0, level, start, masked_thickness(depth_ref, levels_ref, level, start, ROWS))
                put(thick, 1, level, start, rim)

    blocks(load)

    half = 0.5 * time_step
    keep = 1.0 - time_step * drag_rate

    for step in range(STEPS):
        last = step == STEPS - 1

        def winds(start):
            row = lax.broadcasted_iota(jnp.int32, (ROWS, WIDTH), 0) + start
            turn = time_step * (coriolis_base + coriolis_slope * row.astype(jnp.float32) / LAT)
            for level in range(LEV):
                h, u, v, c, t = (
                    [rows_at(ref, side, level, start, 0) for side in range(2)]
                    for ref in (height, zonal, merid, tracer, thick)
                )
                dh = slope(h)
                new_u, new_v, across, down, up = [], [], [], [], []
                for side in range(2):
                    dy = rows_at(height, side, level, start, 1) - rows_at(height, side, level, start, -1)
                    wet = t[side] > 0.0
                    one_u = keep * u[side] + turn * v[side] - (half * gravity) * dh[side]
                    one_v = keep * v[side] - turn * u[side] - (half * gravity) * dy
                    one_u = jnp.where(wet, one_u, 0.0)
                    one_v = jnp.where(wet, one_v, 0.0)
                    some, more = diffusion * c[side], half * c[side]
                    along, cross = more * one_u, more * one_v
                    new_u.append(one_u)
                    new_v.append(one_v)
                    across.append(t[side] * one_u)
                    down.append(some - along)
                    up.append(some + along)
                    if not (last and side):
                        put(flux, side, level, start, t[side] * one_v)
                        put(south, side, level, start, some - cross)
                        put(north, side, level, start, some + cross)
                du = slope(across)
                from_east, from_west = east(down), west(up)
                for side in range(2):
                    if last and side:
                        continue
                    if last:
                        out_ref[LEV + level, pl.ds(start, ROWS), :] = new_u[0]
                        out_ref[2 * LEV + level, pl.ds(start, ROWS), :] = new_v[0]
                    else:
                        put(zonal, side, level, start, new_u[side])
                        put(merid, side, level, start, new_v[side])
                    put(height_part, side, level, start, h[side] - half * du[side])
                    put(
                        tracer, side, level, start,
                        (1.0 - 4.0 * diffusion) * c[side] + (from_east[side] + from_west[side]),
                    )

        def levels(start):
            for side in range(1 if last else 2):
                wets = [rows_at(thick, side, level, start, 0) > 0.0 for level in range(LEV)]
                moved = []
                for level in range(LEV):
                    dy = rows_at(flux, side, level, start, 1) - rows_at(flux, side, level, start, -1)
                    new_h = rows_at(height_part, side, level, start, 0) - half * dy
                    new_h = jnp.where(wets[level], new_h, 0.0)
                    if last:
                        out_ref[level, pl.ds(start, ROWS), :] = new_h
                    else:
                        put(height, side, level, start, new_h)
                    new_c = rows_at(tracer, side, level, start, 0) + (
                        rows_at(south, side, level, start, 1) + rows_at(north, side, level, start, -1)
                    )
                    moved.append(jnp.where(wets[level], new_c, 0.0))
                swaps = [
                    jnp.where(wets[level] & wets[level + 1], vertical_mix * (moved[level + 1] - moved[level]), 0.0)
                    for level in range(LEV - 1)
                ]
                for level in range(LEV):
                    new_c = moved[level]
                    if level < LEV - 1:
                        new_c = new_c + swaps[level]
                    if level > 0:
                        new_c = new_c - swaps[level - 1]
                    if last:
                        out_ref[3 * LEV + level, pl.ds(start, ROWS), :] = new_c
                    else:
                        put(tracer, side, level, start, new_c)

        blocks(winds)
        blocks(levels)


def run_forecast(fields, depth, levels, before, after):
    scratch = pltpu.VMEM((2, LEV, LAT + 2 * PAD, WIDTH), jnp.float32)
    return pl.pallas_call(
        forecast_kernel,
        out_shape=jax.ShapeDtypeStruct(fields.shape, fields.dtype),
        in_specs=vmem(5),
        out_specs=pl.BlockSpec(memory_space=pltpu.VMEM),
        scratch_shapes=[scratch] * 9,
        compiler_params=pltpu.CompilerParams(vmem_limit_bytes=VMEM_LIMIT),
        cost_estimate=pl.CostEstimate(flops=150 * fields.size, bytes_accessed=12 * fields.size, transcendentals=0),
        name="forecast",
    )(fields, depth, levels, before, after)


def ring(values, axis, shift):
    size = lax.axis_size(axis)
    return lax.ppermute(values, axis, [(i, (i + shift) % size) for i in range(size)])


def on_device(state, level_thickness, wet_levels, ancestors):
    size = lax.axis_size("dom")
    own = ancestors.reshape(-1)
    left = ring(own, "lon", 1)
    right = ring(own, "lon", -1)
    chunks = make_chunks(state.reshape(size, -1, WIDTH), own, left, right)
    sent = chunks.reshape(size, -1, 1, WIDTH)
    block = lax.all_to_all(sent, "dom", split_axis=0, concat_axis=0, tiled=True)
    mixed = blend(block.reshape(chunks.shape), size)
    back = lax.all_to_all(mixed, "dom", split_axis=0, concat_axis=0, tiled=True)
    fields = back.reshape(FIELDS * LEV, LAT, WIDTH)
    right, left = pack(fields, level_thickness, wet_levels)
    before = ring(right, "lon", 1)
    after = ring(left, "lon", -1)
    result = run_forecast(fields, level_thickness, wet_levels, before, after)
    return result.reshape(state.shape)


def solution(mesh):
    return jax.shard_map(
        on_device,
        mesh=mesh,
        in_specs=(
            P("dom", None, None, None, "lon"),
            P(None, None, "lon"),
            P(None, "lon"),
            P("dom", "lon", None),
        ),
        out_specs=P("dom", None, None, None, "lon"),
        check_vma=False,
    )
```

```python
import jax
import jax.numpy as jnp
from jax import lax
from jax.experimental import pallas as pl
from jax.experimental.pallas import tpu as pltpu
from jax.sharding import PartitionSpec as P

LEV = 4
FIELDS = 4
TILE = 64
BLEND = 8
STEPS = 3
LAT = 128
WIDTH = 128
HALO = 2 * STEPS
PAD = 8

time_step = 0.3
gravity = 1.0
drag_rate = 0.05
diffusion = 0.1
vertical_mix = 0.2
coriolis_base = 0.1
coriolis_slope = 0.3

VMEM_LIMIT = 16 * 1024 * 1024


def lanes_of(rows):
    return lax.broadcasted_iota(jnp.int32, (rows, WIDTH), 1)


def vmem(count):
    return [pl.BlockSpec(memory_space=pltpu.VMEM)] * count


def chunk_kernel(state_ref, out_ref):
    height = state_ref.shape[1]
    for chunk in range(state_ref.shape[0]):
        base = chunk * (height + 1)
        out_ref[base : base + height, :] = state_ref[chunk]


def make_chunks(chunks):
    count, height, width = chunks.shape
    shape = (count * (height + 1), width)
    return pl.pallas_call(
        chunk_kernel,
        out_shape=jax.ShapeDtypeStruct(shape, chunks.dtype),
        in_specs=vmem(1),
        out_specs=pl.BlockSpec(memory_space=pltpu.VMEM),
        compiler_params=pltpu.CompilerParams(vmem_limit_bytes=VMEM_LIMIT),
        cost_estimate=pl.CostEstimate(flops=0, bytes_accessed=8 * chunks.size, transcendentals=0),
        name="chunks",
    )(chunks)


def add_table(chunks, own, left, right, count):
    height = chunks.shape[0] // count

    def table_kernel(own_ref, left_ref, right_ref, chunks_ref, out_ref):
        del chunks_ref
        lane = lanes_of(1)
        row = jnp.zeros((1, WIDTH), jnp.int32)
        for tile, pick in enumerate((left_ref[1], own_ref[0], own_ref[1], right_ref[0])):
            row = jnp.where(lane == tile, pick, row)
        row = row.astype(jnp.float32)
        for chunk in range(count):
            base = chunk * height + height - 1
            out_ref[base : base + 1, :] = row

    return pl.pallas_call(
        table_kernel,
        out_shape=jax.ShapeDtypeStruct(chunks.shape, chunks.dtype),
        in_specs=[pl.BlockSpec(memory_space=pltpu.SMEM)] * 3 + vmem(1),
        out_specs=pl.BlockSpec(memory_space=pltpu.VMEM),
        input_output_aliases={3: 0},
        compiler_params=pltpu.CompilerParams(vmem_limit_bytes=VMEM_LIMIT),
        cost_estimate=pl.CostEstimate(flops=0, bytes_accessed=4 * count * WIDTH, transcendentals=0),
        name="table",
    )(own, left, right, chunks)


def blend_kernel(block_ref, out_ref, numbers_ref, table_ref, sem):
    particles, rows, _ = out_ref.shape
    numbers_ref[...] = block_ref[pl.ds(rows, particles, stride=rows + 1), :].astype(jnp.int32)
    copy = pltpu.make_async_copy(numbers_ref, table_ref, sem)
    copy.start()
    lane = lanes_of(8)
    position = lane % TILE
    near_left = position < BLEND
    near_right = position >= TILE - BLEND
    distance = jnp.where(near_left, position, TILE - 1 - position).astype(jnp.float32)
    weight = jnp.where(near_left | near_right, 0.5 + (distance + 0.5) / (2.0 * BLEND), 1.0)
    rest = 1.0 - weight
    first = lane < TILE
    zero = jnp.zeros_like(weight)
    weights = (
        jnp.where(first & near_left, rest, zero),
        jnp.where(first, weight, jnp.where(near_left, rest, zero)),
        jnp.where(first, jnp.where(near_right, rest, zero), weight),
        jnp.where(first, zero, jnp.where(near_right, rest, zero)),
    )
    copy.wait()

    def one(particle, carry):
        picks = [table_ref[particle, tile] * (rows + 1) for tile in range(4)]
        for row in range(0, rows, 8):
            parts = [block_ref[pl.ds(pick + row, 8), :] * w for pick, w in zip(picks, weights)]
            out_ref[particle, row : row + 8, :] = (parts[1] + parts[2]) + (parts[0] + parts[3])
        return carry

    lax.fori_loop(0, particles, one, 0, unroll=4)


def blend(block, particles):
    rows = block.shape[0] // particles - 1
    shape = (particles, rows, WIDTH)
    return pl.pallas_call(
        blend_kernel,
        out_shape=jax.ShapeDtypeStruct(shape, block.dtype),
        in_specs=vmem(1),
        out_specs=pl.BlockSpec(memory_space=pltpu.VMEM),
        scratch_shapes=[
            pltpu.VMEM((particles, WIDTH), jnp.int32),
            pltpu.SMEM((particles, WIDTH), jnp.int32),
            pltpu.SemaphoreType.DMA,
        ],
        compiler_params=pltpu.CompilerParams(vmem_limit_bytes=VMEM_LIMIT),
        cost_estimate=pl.CostEstimate(flops=4 * block.size, bytes_accessed=8 * block.size, transcendentals=0),
        name="blend",
    )(block)


def masked_thickness(depth_ref, levels_ref, level, start, rows):
    wet = levels_ref[pl.ds(start, rows), :] > level
    return jnp.where(wet, depth_ref[level, pl.ds(start, rows), :], 0.0)


def groups():
    for kind in range(FIELDS + 1):
        for level in range(LEV):
            yield kind, level, kind * 2 + level % 2, level // 2


def values_of(fields_ref, depth_ref, levels_ref, kind, level, start, rows):
    if kind < FIELDS:
        return fields_ref[kind * LEV + level, pl.ds(start, rows), :]
    return masked_thickness(depth_ref, levels_ref, level, start, rows)


def pack_kernel(fields_ref, depth_ref, levels_ref, right_ref, left_ref):
    lane = lanes_of(8)

    def within(low):
        return ((lane + (WIDTH - low)) % WIDTH) < HALO

    def one(block, carry):
        start = pl.multiple_of(block * 8, 8)
        right = jnp.zeros((8, WIDTH), jnp.float32)
        left = jnp.zeros((8, WIDTH), jnp.float32)
        for kind, level, slot, half in groups():
            values = values_of(fields_ref, depth_ref, levels_ref, kind, level, start, 8)
            low = half * TILE + HALO * slot
            turned = pltpu.roll(values, (low + HALO) % WIDTH, 1)
            right = jnp.where(within(low), turned, right)
            left = jnp.where(within(low + HALO), turned, left)
        right_ref[pl.ds(start, 8), :] = right
        left_ref[pl.ds(start, 8), :] = left
        return carry

    lax.fori_loop(0, LAT // 8, one, 0, unroll=4)


def pack(fields, depth, levels):
    shape = jax.ShapeDtypeStruct((LAT, WIDTH), jnp.float32)
    return pl.pallas_call(
        pack_kernel,
        out_shape=(shape, shape),
        in_specs=vmem(3),
        out_specs=tuple(vmem(2)),
        compiler_params=pltpu.CompilerParams(vmem_limit_bytes=VMEM_LIMIT),
        cost_estimate=pl.CostEstimate(flops=4 * fields.size, bytes_accessed=5 * fields.size, transcendentals=0),
        name="pack",
    )(fields, depth, levels)


def march(scratch, count, couple, emit):
    height, zonal, merid, tracer, thick, height_part, flux, south, north = scratch

    def rows_at(ref, which, shift):
        return ref[which, PAD + shift : PAD + LAT + shift, :]

    def put(ref, which, values):
        ref[which, PAD : PAD + LAT, :] = values

    def east(values):
        return pltpu.roll(values, WIDTH - 1, 1)

    def west(values):
        return pltpu.roll(values, 1, 1)

    edge = jnp.zeros((PAD, WIDTH), jnp.float32)
    for ref in (height, flux, south, north):
        for which in range(count):
            ref[which, 0:PAD, :] = edge
            ref[which, PAD + LAT : 2 * PAD + LAT, :] = edge

    half = 0.5 * time_step
    keep = 1.0 - time_step * drag_rate
    row = lax.broadcasted_iota(jnp.int32, (LAT, WIDTH), 0)
    turn = time_step * (coriolis_base + coriolis_slope * row.astype(jnp.float32) / LAT)

    for step in range(STEPS):
        last = step == STEPS - 1
        for which in range(count):
            h, u, v, c, t = (rows_at(ref, which, 0) for ref in (height, zonal, merid, tracer, thick))
            wet = t > 0.0
            dx = east(h) - west(h)
            dy = rows_at(height, which, 1) - rows_at(height, which, -1)
            new_u = jnp.where(wet, keep * u + turn * v - (half * gravity) * dx, 0.0)
            new_v = jnp.where(wet, keep * v - turn * u - (half * gravity) * dy, 0.0)
            some, more = diffusion * c, half * c
            along, cross = more * new_u, more * new_v
            across = t * new_u
            put(flux, which, t * new_v)
            put(south, which, some - cross)
            put(north, which, some + cross)
            if last:
                emit(1, which, new_u)
                emit(2, which, new_v)
            else:
                put(zonal, which, new_u)
                put(merid, which, new_v)
            put(height_part, which, h - half * (east(across) - west(across)))
            put(tracer, which, (1.0 - 4.0 * diffusion) * c + (east(some - along) + west(some + along)))
        moved, wets = [], []
        for which in range(count):
            wet = rows_at(thick, which, 0) > 0.0
            dy = rows_at(flux, which, 1) - rows_at(flux, which, -1)
            new_h = jnp.where(wet, rows_at(height_part, which, 0) - half * dy, 0.0)
            if last:
                emit(0, which, new_h)
            else:
                put(height, which, new_h)
            new_c = rows_at(tracer, which, 0) + (rows_at(south, which, 1) + rows_at(north, which, -1))
            moved.append(jnp.where(wet, new_c, 0.0))
            wets.append(wet)
        for which, new_c in enumerate(couple(moved, wets)):
            if last:
                emit(3, which, new_c)
            else:
                put(tracer, which, new_c)


def exchange(upper, lower, both_wet):
    return jnp.where(both_wet, vertical_mix * (lower - upper), 0.0)


def couple_levels(moved, wets):
    swaps = [exchange(moved[k], moved[k + 1], wets[k] & wets[k + 1]) for k in range(LEV - 1)]
    return [
        moved[0] + swaps[0],
        moved[1] + swaps[1] - swaps[0],
        moved[2] + swaps[2] - swaps[1],
        moved[3] - swaps[2],
    ]


def couple_pairs(moved, wets):
    even, odd = moved
    within = exchange(even, odd, wets[0] & wets[1])
    lane = lanes_of(LAT)
    wet_even = jnp.where(wets[0], 1.0, 0.0)
    turned = pltpu.roll(even, TILE, 1)
    turned_wet = pltpu.roll(wet_even, TILE, 1) > 0.0
    between = exchange(odd, turned, wets[1] & turned_wet & (lane < TILE))
    return [even + within - pltpu.roll(between, TILE, 1), odd + between - within]


def scratch_for(count):
    return [pltpu.VMEM((count, LAT + 2 * PAD, WIDTH), jnp.float32)] * 9


STRIP = 2 * HALO


def inner_kernel(fields_ref, depth_ref, levels_ref, out_ref, strip_ref, *scratch):
    lane = lanes_of(LAT)
    for kind, level, slot, half in groups():
        values = values_of(fields_ref, depth_ref, levels_ref, kind, level, 0, LAT)
        scratch[kind][level, PAD : PAD + LAT, :] = values
        base = half * TILE
        ends = jnp.where(
            lane < base + 24, pltpu.roll(values, base + STRIP, 1), pltpu.roll(values, base + 2 * STRIP, 1)
        )
        if half:
            strip_ref[slot] = jnp.where(lane < TILE, strip_ref[slot], ends)
        else:
            strip_ref[slot] = ends

    def emit(kind, level, values):
        out_ref[kind * LEV + level] = values

    march(scratch, LEV, couple_levels, emit)


def run_inner(fields, depth, levels):
    return pl.pallas_call(
        inner_kernel,
        out_shape=(
            jax.ShapeDtypeStruct(fields.shape, fields.dtype),
            jax.ShapeDtypeStruct((2 * (FIELDS + 1), LAT, WIDTH), fields.dtype),
        ),
        in_specs=vmem(3),
        out_specs=tuple(vmem(2)),
        scratch_shapes=scratch_for(LEV),
        compiler_params=pltpu.CompilerParams(vmem_limit_bytes=VMEM_LIMIT),
        cost_estimate=pl.CostEstimate(flops=75 * fields.size, bytes_accessed=12 * fields.size, transcendentals=0),
        name="inner",
    )(fields, depth, levels)


def ends_kernel(inner_ref, strip_ref, before_ref, after_ref, out_ref, *scratch):
    lane = lanes_of(LAT)
    place = lane % TILE
    in_after = (place >= STRIP) & (place < STRIP + HALO)
    in_before = (place >= STRIP + HALO) & (place < 2 * STRIP)
    before = before_ref[...]
    after = after_ref[...]
    for kind in range(FIELDS + 1):
        for which in range(2):
            slot = kind * 2 + which
            low = HALO * slot
            values = jnp.where(
                in_after,
                pltpu.roll(after, (WIDTH + STRIP - low - HALO) % WIDTH, 1),
                jnp.where(
                    in_before, pltpu.roll(before, (WIDTH + STRIP + HALO - low) % WIDTH, 1), strip_ref[slot]
                ),
            )
            scratch[kind][which, PAD : PAD + LAT, :] = values

    def emit(kind, which, values):
        for half in range(2):
            base = half * TILE
            at = kind * LEV + which + 2 * half
            last_columns = pltpu.roll(values, (WIDTH - STRIP - base) % WIDTH, 1)
            first_columns = pltpu.roll(values, (2 * WIDTH - base - 2 * STRIP) % WIDTH, 1)
            out_ref[at] = jnp.where(
                lane < HALO, first_columns, jnp.where(lane >= WIDTH - HALO, last_columns, inner_ref[at])
            )

    march(scratch, 2, couple_pairs, emit)


def run_ends(inner, strips, before, after):
    return pl.pallas_call(
        ends_kernel,
        out_shape=jax.ShapeDtypeStruct(inner.shape, inner.dtype),
        in_specs=vmem(4),
        out_specs=pl.BlockSpec(memory_space=pltpu.VMEM),
        scratch_shapes=scratch_for(2),
        compiler_params=pltpu.CompilerParams(vmem_limit_bytes=VMEM_LIMIT),
        cost_estimate=pl.CostEstimate(flops=40 * inner.size, bytes_accessed=12 * inner.size, transcendentals=0),
        name="ends",
    )(inner, strips, before, after)


def run_forecast(fields, depth, levels, before, after):
    inner, strips = run_inner(fields, depth, levels)
    return run_ends(inner, strips, before, after)


def ring(values, axis, shift):
    size = lax.axis_size(axis)
    return lax.ppermute(values, axis, [(i, (i + shift) % size) for i in range(size)])


def on_device(state, level_thickness, wet_levels, ancestors):
    size = lax.axis_size("dom")
    own = ancestors.reshape(-1)
    left = ring(own, "lon", 1)
    right = ring(own, "lon", -1)
    chunks = make_chunks(state.reshape(size, -1, WIDTH))
    chunks = add_table(chunks, own, left, right, size)
    sent = chunks.reshape(size, -1, 1, WIDTH)
    block = lax.all_to_all(sent, "dom", split_axis=0, concat_axis=0, tiled=True)
    mixed = blend(block.reshape(chunks.shape), size)
    back = lax.all_to_all(mixed, "dom", split_axis=0, concat_axis=0, tiled=True)
    fields = back.reshape(FIELDS * LEV, LAT, WIDTH)
    right, left = pack(fields, level_thickness, wet_levels)
    before = ring(right, "lon", 1)
    after = ring(left, "lon", -1)
    result = run_forecast(fields, level_thickness, wet_levels, before, after)
    return result.reshape(state.shape)


def solution(mesh):
    return jax.shard_map(
        on_device,
        mesh=mesh,
        in_specs=(
            P("dom", None, None, None, "lon"),
            P(None, None, "lon"),
            P(None, "lon"),
            P("dom", "lon", None),
        ),
        out_specs=P("dom", None, None, None, "lon"),
        check_vma=False,
    )
```

```python
import jax
import jax.numpy as jnp
from jax import lax
from jax.experimental import pallas as pl
from jax.experimental.pallas import tpu as pltpu
from jax.sharding import PartitionSpec as P

LEV = 4
FIELDS = 4
TILE = 64
BLEND = 8
STEPS = 3
LAT = 128
WIDTH = 128
HALO = 2 * STEPS
PAD = 8

time_step = 0.3
gravity = 1.0
drag_rate = 0.05
diffusion = 0.1
vertical_mix = 0.2
coriolis_base = 0.1
coriolis_slope = 0.3

VMEM_LIMIT = 16 * 1024 * 1024


def lanes_of(rows):
    return lax.broadcasted_iota(jnp.int32, (rows, WIDTH), 1)


def vmem(count):
    return [pl.BlockSpec(memory_space=pltpu.VMEM)] * count


def chunk_kernel(state_ref, out_ref):
    height = state_ref.shape[1]
    for chunk in range(state_ref.shape[0]):
        base = chunk * (height + 1)
        out_ref[base : base + height, :] = state_ref[chunk]


def make_chunks(chunks):
    count, height, width = chunks.shape
    shape = (count * (height + 1), width)
    return pl.pallas_call(
        chunk_kernel,
        out_shape=jax.ShapeDtypeStruct(shape, chunks.dtype),
        in_specs=vmem(1),
        out_specs=pl.BlockSpec(memory_space=pltpu.VMEM),
        compiler_params=pltpu.CompilerParams(vmem_limit_bytes=VMEM_LIMIT),
        cost_estimate=pl.CostEstimate(flops=0, bytes_accessed=8 * chunks.size, transcendentals=0),
        name="chunks",
    )(chunks)


def add_table(chunks, own, left, right, count):
    height = chunks.shape[0] // count

    def table_kernel(own_ref, left_ref, right_ref, chunks_ref, out_ref):
        del chunks_ref
        tile = lanes_of(1) % 4
        picks = (left_ref[0:1, 1:2], own_ref[0:1, 0:1], own_ref[0:1, 1:2], right_ref[0:1, 0:1])
        row = jnp.zeros((1, WIDTH), jnp.int32)
        for at, pick in enumerate(picks):
            row = jnp.where(tile == at, pick, row)
        row = row.astype(jnp.float32)
        for chunk in range(count):
            base = chunk * height + height - 1
            out_ref[base : base + 1, :] = row

    return pl.pallas_call(
        table_kernel,
        out_shape=jax.ShapeDtypeStruct(chunks.shape, chunks.dtype),
        in_specs=vmem(4),
        out_specs=pl.BlockSpec(memory_space=pltpu.VMEM),
        input_output_aliases={3: 0},
        compiler_params=pltpu.CompilerParams(vmem_limit_bytes=VMEM_LIMIT),
        cost_estimate=pl.CostEstimate(flops=0, bytes_accessed=4 * count * WIDTH, transcendentals=0),
        name="table",
    )(own, left, right, chunks)


SHARE = WIDTH // 4


def blend_kernel(block_ref, out_ref, numbers_ref, table_ref, sem):
    particles, rows, _ = out_ref.shape
    table = block_ref[pl.ds(rows, particles, stride=rows + 1), :]
    holder = lax.broadcasted_iota(jnp.int32, (particles, WIDTH), 0) % SHARE
    table = jnp.where(lanes_of(particles) // 4 == holder, table, 0.0)
    for line in range(particles // SHARE):
        total = jnp.sum(table[line * SHARE : (line + 1) * SHARE], axis=0, keepdims=True)
        numbers_ref[line : line + 1, :] = total.astype(jnp.int32)
    copy = pltpu.make_async_copy(numbers_ref, table_ref, sem)
    copy.start()
    lane = lanes_of(8)
    position = lane % TILE
    near_left = position < BLEND
    near_right = position >= TILE - BLEND
    distance = jnp.where(near_left, position, TILE - 1 - position).astype(jnp.float32)
    weight = jnp.where(near_left | near_right, 0.5 + (distance + 0.5) / (2.0 * BLEND), 1.0)
    rest = 1.0 - weight
    first = lane < TILE
    zero = jnp.zeros_like(weight)
    weights = (
        jnp.where(first & near_left, rest, zero),
        jnp.where(first, weight, jnp.where(near_left, rest, zero)),
        jnp.where(first, jnp.where(near_right, rest, zero), weight),
        jnp.where(first, zero, jnp.where(near_right, rest, zero)),
    )
    copy.wait()

    def one(particle, carry):
        line, first_tile = particle // SHARE, 4 * (particle % SHARE)
        picks = [table_ref[line, first_tile + tile] * (rows + 1) for tile in range(4)]
        for row in range(0, rows, 8):
            parts = [block_ref[pl.ds(pick + row, 8), :] * w for pick, w in zip(picks, weights)]
            out_ref[particle, row : row + 8, :] = (parts[1] + parts[2]) + (parts[0] + parts[3])
        return carry

    lax.fori_loop(0, particles, one, 0, unroll=4)


def blend(block, particles):
    rows = block.shape[0] // particles - 1
    shape = (particles, rows, WIDTH)
    return pl.pallas_call(
        blend_kernel,
        out_shape=jax.ShapeDtypeStruct(shape, block.dtype),
        in_specs=vmem(1),
        out_specs=pl.BlockSpec(memory_space=pltpu.VMEM),
        scratch_shapes=[
            pltpu.VMEM((particles // SHARE, WIDTH), jnp.int32),
            pltpu.SMEM((particles // SHARE, WIDTH), jnp.int32),
            pltpu.SemaphoreType.DMA,
        ],
        compiler_params=pltpu.CompilerParams(vmem_limit_bytes=VMEM_LIMIT),
        cost_estimate=pl.CostEstimate(flops=4 * block.size, bytes_accessed=8 * block.size, transcendentals=0),
        name="blend",
    )(block)


def masked_thickness(depth_ref, levels_ref, level, start, rows):
    wet = levels_ref[pl.ds(start, rows), :] > level
    return jnp.where(wet, depth_ref[level, pl.ds(start, rows), :], 0.0)


def groups():
    for kind in range(FIELDS + 1):
        for level in range(LEV):
            yield kind, level, kind * 2 + level % 2, level // 2


def values_of(fields_ref, depth_ref, levels_ref, kind, level, start, rows):
    if kind < FIELDS:
        return fields_ref[kind * LEV + level, pl.ds(start, rows), :]
    return masked_thickness(depth_ref, levels_ref, level, start, rows)


def pack_kernel(fields_ref, depth_ref, levels_ref, right_ref, left_ref):
    lane = lanes_of(PROWS)

    def within(low):
        return ((lane + (WIDTH - low)) % WIDTH) < HALO

    for start in range(0, LAT, PROWS):
        right = jnp.zeros((PROWS, WIDTH), jnp.float32)
        left = jnp.zeros((PROWS, WIDTH), jnp.float32)
        for kind, level, slot, half in groups():
            values = values_of(fields_ref, depth_ref, levels_ref, kind, level, start, PROWS)
            low = half * TILE + HALO * slot
            turned = pltpu.roll(values, (low + HALO) % WIDTH, 1)
            right = jnp.where(within(low), turned, right)
            left = jnp.where(within(low + HALO), turned, left)
        right_ref[start : start + PROWS, :] = right
        left_ref[start : start + PROWS, :] = left


def pack(fields, depth, levels):
    shape = jax.ShapeDtypeStruct((LAT, WIDTH), jnp.float32)
    return pl.pallas_call(
        pack_kernel,
        out_shape=(shape, shape),
        in_specs=vmem(3),
        out_specs=tuple(vmem(2)),
        compiler_params=pltpu.CompilerParams(vmem_limit_bytes=VMEM_LIMIT),
        cost_estimate=pl.CostEstimate(flops=4 * fields.size, bytes_accessed=5 * fields.size, transcendentals=0),
        name="pack",
    )(fields, depth, levels)


def march(scratch, count, couple, emit, winds_done=lambda: None):
    height, zonal, merid, tracer, thick, flux, south, north = scratch

    def rows_at(ref, shift):
        return ref[:, PAD + shift : PAD + LAT + shift, :]

    def put(ref, values):
        ref[:, PAD : PAD + LAT, :] = values

    def east(values):
        return pltpu.roll(values, WIDTH - 1, 2)

    def west(values):
        return pltpu.roll(values, 1, 2)

    edge = jnp.zeros((count, PAD, WIDTH), jnp.float32)
    for ref in (height, flux, south, north):
        ref[:, 0:PAD, :] = edge
        ref[:, PAD + LAT : 2 * PAD + LAT, :] = edge

    half = 0.5 * time_step
    keep = 1.0 - time_step * drag_rate
    row = lax.broadcasted_iota(jnp.int32, (LAT, WIDTH), 0)
    turn = time_step * (coriolis_base + coriolis_slope * row.astype(jnp.float32) / LAT)
    turn = turn[None]

    for step in range(STEPS):
        last = step == STEPS - 1
        h, u, v, c, t = (rows_at(ref, 0) for ref in (height, zonal, merid, tracer, thick))
        wet = t > 0.0
        dx = east(h) - west(h)
        dy = rows_at(height, 1) - rows_at(height, -1)
        new_u = jnp.where(wet, keep * u + turn * v - (half * gravity) * dx, 0.0)
        new_v = jnp.where(wet, keep * v - turn * u - (half * gravity) * dy, 0.0)
        some, more = diffusion * c, half * c
        along, cross = more * new_u, more * new_v
        across = t * new_u
        put(flux, t * new_v)
        put(south, some - cross)
        put(north, some + cross)
        if last:
            for which in range(count):
                emit(1, which, new_u[which])
                emit(2, which, new_v[which])
            winds_done()
        else:
            put(zonal, new_u)
            put(merid, new_v)
        part = h - half * (east(across) - west(across))
        c_part = (1.0 - 4.0 * diffusion) * c + (east(some - along) + west(some + along))
        dy = rows_at(flux, 1) - rows_at(flux, -1)
        new_h = jnp.where(wet, part - half * dy, 0.0)
        new_c = jnp.where(wet, c_part + (rows_at(south, 1) + rows_at(north, -1)), 0.0)
        moved = [new_c[which] for which in range(count)]
        wets = [wet[which] for which in range(count)]
        coupled = couple(moved, wets)
        for which in range(count):
            if last:
                emit(0, which, new_h[which])
                emit(3, which, coupled[which])
            else:
                height[which, PAD : PAD + LAT, :] = new_h[which]
                tracer[which, PAD : PAD + LAT, :] = coupled[which]


def exchange(upper, lower, both_wet):
    return jnp.where(both_wet, vertical_mix * (lower - upper), 0.0)


def couple_levels(moved, wets):
    swaps = [exchange(moved[k], moved[k + 1], wets[k] & wets[k + 1]) for k in range(LEV - 1)]
    return [
        moved[0] + swaps[0],
        moved[1] + swaps[1] - swaps[0],
        moved[2] + swaps[2] - swaps[1],
        moved[3] - swaps[2],
    ]


def couple_pairs(moved, wets):
    even, odd = moved
    within = exchange(even, odd, wets[0] & wets[1])
    lane = lanes_of(LAT)
    wet_even = jnp.where(wets[0], 1.0, 0.0)
    turned = pltpu.roll(even, TILE, 1)
    turned_wet = pltpu.roll(wet_even, TILE, 1) > 0.0
    between = exchange(odd, turned, wets[1] & turned_wet & (lane < TILE))
    return [even + within - pltpu.roll(between, TILE, 1), odd + between - within]


def scratch_for(count):
    return [pltpu.VMEM((count, LAT + 2 * PAD, WIDTH), jnp.float32)] * 8


STRIP = 2 * HALO
PROWS = 128


def inner_kernel(fields_ref, depth_ref, levels_ref, out_ref, strip_ref, *scratch):
    lane = lanes_of(LAT)
    for kind, level, slot, half in groups():
        values = values_of(fields_ref, depth_ref, levels_ref, kind, level, 0, LAT)
        scratch[kind][level, PAD : PAD + LAT, :] = values
        base = half * TILE
        ends = jnp.where(
            lane < base + 24, pltpu.roll(values, base + STRIP, 1), pltpu.roll(values, base + 2 * STRIP, 1)
        )
        if half:
            strip_ref[slot] = jnp.where(lane < TILE, strip_ref[slot], ends)
        else:
            strip_ref[slot] = ends

    def emit(kind, level, values):
        out_ref[kind * LEV + level] = values

    march(scratch, LEV, couple_levels, emit)


def run_inner(fields, depth, levels):
    return pl.pallas_call(
        inner_kernel,
        out_shape=(
            jax.ShapeDtypeStruct(fields.shape, fields.dtype),
            jax.ShapeDtypeStruct((2 * (FIELDS + 1), LAT, WIDTH), fields.dtype),
        ),
        in_specs=vmem(3),
        out_specs=tuple(vmem(2)),
        scratch_shapes=scratch_for(LEV),
        compiler_params=pltpu.CompilerParams(vmem_limit_bytes=VMEM_LIMIT),
        cost_estimate=pl.CostEstimate(flops=75 * fields.size, bytes_accessed=12 * fields.size, transcendentals=0),
        name="inner",
    )(fields, depth, levels)


def ends_kernel(inner_ref, strip_ref, before_ref, after_ref, out_ref, result_ref, sems, *scratch):
    lane = lanes_of(LAT)
    place = lane % TILE
    in_after = (place >= STRIP) & (place < STRIP + HALO)
    in_before = (place >= STRIP + HALO) & (place < 2 * STRIP)
    before = before_ref[...]
    after = after_ref[...]
    for kind in range(FIELDS + 1):
        for which in range(2):
            slot = kind * 2 + which
            low = HALO * slot
            values = jnp.where(
                in_after,
                pltpu.roll(after, (WIDTH + STRIP - low - HALO) % WIDTH, 1),
                jnp.where(
                    in_before, pltpu.roll(before, (WIDTH + STRIP + HALO - low) % WIDTH, 1), strip_ref[slot]
                ),
            )
            scratch[kind][which, PAD : PAD + LAT, :] = values

    def emit(kind, which, values):
        for half in range(2):
            base = half * TILE
            at = kind * LEV + which + 2 * half
            last_columns = pltpu.roll(values, (WIDTH - STRIP - base) % WIDTH, 1)
            first_columns = pltpu.roll(values, (2 * WIDTH - base - 2 * STRIP) % WIDTH, 1)
            result_ref[at] = jnp.where(
                lane < HALO, first_columns, jnp.where(lane >= WIDTH - HALO, last_columns, inner_ref[at])
            )

    copies = [
        pltpu.make_async_copy(
            result_ref.at[kind * LEV : kind * LEV + LEV], out_ref.at[kind * LEV : kind * LEV + LEV], sems.at[kind]
        )
        for kind in range(FIELDS)
    ]

    def winds_done():
        copies[1].start()
        copies[2].start()

    march(scratch, 2, couple_pairs, emit, winds_done)
    copies[0].start()
    copies[3].start()
    for copy in copies:
        copy.wait()


def run_ends(inner, strips, before, after):
    return pl.pallas_call(
        ends_kernel,
        out_shape=jax.ShapeDtypeStruct(inner.shape, inner.dtype),
        in_specs=vmem(4),
        out_specs=pl.BlockSpec(memory_space=pl.ANY),
        scratch_shapes=[pltpu.VMEM(inner.shape, inner.dtype), pltpu.SemaphoreType.DMA((FIELDS,))] + scratch_for(2),
        compiler_params=pltpu.CompilerParams(vmem_limit_bytes=VMEM_LIMIT),
        cost_estimate=pl.CostEstimate(flops=40 * inner.size, bytes_accessed=12 * inner.size, transcendentals=0),
        name="ends",
    )(inner, strips, before, after)


def run_forecast(fields, depth, levels, before, after):
    inner, strips = run_inner(fields, depth, levels)
    return run_ends(inner, strips, before, after)


def ring(values, axis, shift):
    size = lax.axis_size(axis)
    return lax.ppermute(values, axis, [(i, (i + shift) % size) for i in range(size)])


def on_device(state, level_thickness, wet_levels, ancestors):
    size = lax.axis_size("dom")
    own = ancestors.reshape(1, -1)
    left = ring(own, "lon", 1)
    right = ring(own, "lon", -1)
    chunks = make_chunks(state.reshape(size, -1, WIDTH))
    chunks = add_table(chunks, own, left, right, size)
    sent = chunks.reshape(size, -1, 1, WIDTH)
    block = lax.all_to_all(sent, "dom", split_axis=0, concat_axis=0, tiled=True)
    mixed = blend(block.reshape(chunks.shape), size)
    back = lax.all_to_all(mixed, "dom", split_axis=0, concat_axis=0, tiled=True)
    fields = back.reshape(FIELDS * LEV, LAT, WIDTH)
    right, left = pack(fields, level_thickness, wet_levels)
    before = ring(right, "lon", 1)
    after = ring(left, "lon", -1)
    result = run_forecast(fields, level_thickness, wet_levels, before, after)
    return result.reshape(state.shape)


def solution(mesh):
    return jax.shard_map(
        on_device,
        mesh=mesh,
        in_specs=(
            P("dom", None, None, None, "lon"),
            P(None, None, "lon"),
            P(None, "lon"),
            P("dom", "lon", None),
        ),
        out_specs=P("dom", None, None, None, "lon"),
        check_vma=False,
    )
```

```python
import jax
import jax.numpy as jnp
from jax import lax
from jax.experimental import pallas as pl
from jax.experimental.pallas import tpu as pltpu
from jax.sharding import PartitionSpec as P

LEV = 4
FIELDS = 4
TILE = 64
BLEND = 8
STEPS = 3
LAT = 128
WIDTH = 128
HALO = 2 * STEPS
DOM = (2, 4, 8)
HOP = (1, 2, 4)
PAD = 8

time_step = 0.3
gravity = 1.0
drag_rate = 0.05
diffusion = 0.1
vertical_mix = 0.2
coriolis_base = 0.1
coriolis_slope = 0.3

VMEM_LIMIT = 16 * 1024 * 1024


def lanes_of(rows):
    return lax.broadcasted_iota(jnp.int32, (rows, WIDTH), 1)


def vmem(count):
    return [pl.BlockSpec(memory_space=pltpu.VMEM)] * count


def chunk_kernel(state_ref, out_ref):
    height = state_ref.shape[1]
    for chunk in range(state_ref.shape[0]):
        base = chunk * (height + 1)
        out_ref[base : base + height, :] = state_ref[chunk]


def make_chunks(chunks):
    count, height, width = chunks.shape
    shape = (count * (height + 1), width)
    return pl.pallas_call(
        chunk_kernel,
        out_shape=jax.ShapeDtypeStruct(shape, chunks.dtype),
        in_specs=vmem(1),
        out_specs=pl.BlockSpec(memory_space=pltpu.VMEM),
        compiler_params=pltpu.CompilerParams(vmem_limit_bytes=VMEM_LIMIT),
        cost_estimate=pl.CostEstimate(flops=0, bytes_accessed=8 * chunks.size, transcendentals=0),
        name="chunks",
    )(chunks)


def add_table(chunks, own, left, right, turn, count):
    height = chunks.shape[0] // count

    def table_kernel(own_ref, left_ref, right_ref, turn_ref, chunks_ref, out_ref):
        del turn_ref, chunks_ref
        tile = lanes_of(1) % 4
        picks = (left_ref[0:1, 1:2], own_ref[0:1, 0:1], own_ref[0:1, 1:2], right_ref[0:1, 0:1])
        row = jnp.zeros((1, WIDTH), jnp.int32)
        for at, pick in enumerate(picks):
            row = jnp.where(tile == at, pick, row)
        row = row.astype(jnp.float32)
        for chunk in range(count):
            base = chunk * height + height - 1
            out_ref[base : base + 1, :] = row

    return pl.pallas_call(
        table_kernel,
        out_shape=jax.ShapeDtypeStruct(chunks.shape, chunks.dtype),
        in_specs=vmem(5),
        out_specs=pl.BlockSpec(memory_space=pltpu.VMEM),
        input_output_aliases={4: 0},
        compiler_params=pltpu.CompilerParams(vmem_limit_bytes=VMEM_LIMIT),
        cost_estimate=pl.CostEstimate(flops=0, bytes_accessed=4 * count * WIDTH, transcendentals=0),
        name="table",
    )(own, left, right, turn, chunks)


SHARE = WIDTH // 4
TOGETHER = 8
BROWS = 32
UNROLL = 2


def blend_kernel(block_ref, out_ref, numbers_ref, table_ref, sem):
    particles, rows, _ = out_ref.shape
    table = block_ref[pl.ds(rows, particles, stride=rows + 1), :]
    holder = lax.broadcasted_iota(jnp.int32, (particles, WIDTH), 0) % SHARE
    table = jnp.where(lanes_of(particles) // 4 == holder, table, 0.0)
    for line in range(particles // SHARE):
        total = jnp.sum(table[line * SHARE : (line + 1) * SHARE], axis=0, keepdims=True)
        numbers_ref[line : line + 1, :] = total.astype(jnp.int32)
    copy = pltpu.make_async_copy(numbers_ref, table_ref, sem)
    copy.start()
    lane = lanes_of(BROWS)
    position = lane % TILE
    near_left = position < BLEND
    near_right = position >= TILE - BLEND
    distance = jnp.where(near_left, position, TILE - 1 - position).astype(jnp.float32)
    weight = jnp.where(near_left | near_right, 0.5 + (distance + 0.5) / (2.0 * BLEND), 1.0)
    rest = 1.0 - weight
    first = lane < TILE
    zero = jnp.zeros_like(weight)
    weights = (
        jnp.where(first & near_left, rest, zero),
        jnp.where(first, weight, jnp.where(near_left, rest, zero)),
        jnp.where(first, jnp.where(near_right, rest, zero), weight),
        jnp.where(first, zero, jnp.where(near_right, rest, zero)),
    )
    copy.wait()

    def some(at, carry):
        done = []
        for particle in range(TOGETHER):
            particle = at * TOGETHER + particle
            line, first_tile = particle // SHARE, 4 * (particle % SHARE)
            picks = [table_ref[line, first_tile + tile] * (rows + 1) for tile in range(4)]
            for row in range(0, rows, BROWS):
                parts = [block_ref[pl.ds(pick + row, BROWS), :] * w for pick, w in zip(picks, weights)]
                done.append((particle, row, (parts[1] + parts[2]) + (parts[0] + parts[3])))
        for particle, row, values in done:
            out_ref[particle, row : row + BROWS, :] = values
        return carry

    lax.fori_loop(0, particles // TOGETHER, some, 0, unroll=UNROLL)


def blend(block, particles):
    rows = block.shape[0] // particles - 1
    shape = (particles, rows, WIDTH)
    return pl.pallas_call(
        blend_kernel,
        out_shape=jax.ShapeDtypeStruct(shape, block.dtype),
        in_specs=vmem(1),
        out_specs=pl.BlockSpec(memory_space=pltpu.VMEM),
        scratch_shapes=[
            pltpu.VMEM((particles // SHARE, WIDTH), jnp.int32),
            pltpu.SMEM((particles // SHARE, WIDTH), jnp.int32),
            pltpu.SemaphoreType.DMA,
        ],
        compiler_params=pltpu.CompilerParams(vmem_limit_bytes=VMEM_LIMIT),
        cost_estimate=pl.CostEstimate(flops=4 * block.size, bytes_accessed=8 * block.size, transcendentals=0),
        name="blend",
    )(block)


def masked_thickness(depth_ref, levels_ref, level, start, rows):
    wet = levels_ref[pl.ds(start, rows), :] > level
    return jnp.where(wet, depth_ref[level, pl.ds(start, rows), :], 0.0)


def groups():
    for kind in range(FIELDS + 1):
        for level in range(LEV):
            yield kind, level, kind * 2 + level % 2, level // 2


def values_of(fields_ref, depth_ref, levels_ref, kind, level, start, rows):
    if kind < FIELDS:
        return fields_ref[kind * LEV + level, pl.ds(start, rows), :]
    return masked_thickness(depth_ref, levels_ref, level, start, rows)


def pack_kernel(fields_ref, depth_ref, levels_ref, right_ref, left_ref):
    lane = lanes_of(PROWS)

    def within(low):
        return ((lane + (WIDTH - low)) % WIDTH) < HALO

    for start in range(0, LAT, PROWS):
        right = jnp.zeros((PROWS, WIDTH), jnp.float32)
        left = jnp.zeros((PROWS, WIDTH), jnp.float32)
        for kind, level, slot, half in groups():
            values = values_of(fields_ref, depth_ref, levels_ref, kind, level, start, PROWS)
            low = half * TILE + HALO * slot
            turned = pltpu.roll(values, (low + HALO) % WIDTH, 1)
            right = jnp.where(within(low), turned, right)
            left = jnp.where(within(low + HALO), turned, left)
        right_ref[start : start + PROWS, :] = right
        left_ref[start : start + PROWS, :] = left


def pack(fields, depth, levels):
    shape = jax.ShapeDtypeStruct((LAT, WIDTH), jnp.float32)
    return pl.pallas_call(
        pack_kernel,
        out_shape=(shape, shape),
        in_specs=vmem(3),
        out_specs=tuple(vmem(2)),
        compiler_params=pltpu.CompilerParams(vmem_limit_bytes=VMEM_LIMIT),
        cost_estimate=pl.CostEstimate(flops=4 * fields.size, bytes_accessed=5 * fields.size, transcendentals=0),
        name="pack",
    )(fields, depth, levels)


def march(scratch, count, couple, emit, winds_done=lambda: None):
    height, zonal, merid, tracer, thick, flux, south, north = scratch

    def rows_at(ref, shift):
        return ref[:, PAD + shift : PAD + LAT + shift, :]

    def put(ref, values):
        ref[:, PAD : PAD + LAT, :] = values

    def east(values):
        return pltpu.roll(values, WIDTH - 1, 2)

    def west(values):
        return pltpu.roll(values, 1, 2)

    edge = jnp.zeros((count, PAD, WIDTH), jnp.float32)
    for ref in (height, flux, south, north):
        ref[:, 0:PAD, :] = edge
        ref[:, PAD + LAT : 2 * PAD + LAT, :] = edge

    half = 0.5 * time_step
    keep = 1.0 - time_step * drag_rate
    row = lax.broadcasted_iota(jnp.int32, (LAT, WIDTH), 0)
    turn = time_step * (coriolis_base + coriolis_slope * row.astype(jnp.float32) / LAT)
    turn = turn[None]

    for step in range(STEPS):
        last = step == STEPS - 1
        h, u, v, c, t = (rows_at(ref, 0) for ref in (height, zonal, merid, tracer, thick))
        wet = t > 0.0
        dx = east(h) - west(h)
        dy = rows_at(height, 1) - rows_at(height, -1)
        new_u = jnp.where(wet, keep * u + turn * v - (half * gravity) * dx, 0.0)
        new_v = jnp.where(wet, keep * v - turn * u - (half * gravity) * dy, 0.0)
        some, more = diffusion * c, half * c
        along, cross = more * new_u, more * new_v
        across = t * new_u
        put(flux, t * new_v)
        put(south, some - cross)
        put(north, some + cross)
        if last:
            for which in range(count):
                emit(1, which, new_u[which])
                emit(2, which, new_v[which])
            winds_done()
        else:
            put(zonal, new_u)
            put(merid, new_v)
        part = h - half * (east(across) - west(across))
        c_part = (1.0 - 4.0 * diffusion) * c + (east(some - along) + west(some + along))
        dy = rows_at(flux, 1) - rows_at(flux, -1)
        new_h = jnp.where(wet, part - half * dy, 0.0)
        new_c = jnp.where(wet, c_part + (rows_at(south, 1) + rows_at(north, -1)), 0.0)
        moved = [new_c[which] for which in range(count)]
        wets = [wet[which] for which in range(count)]
        coupled = couple(moved, wets)
        for which in range(count):
            if last:
                emit(0, which, new_h[which])
                emit(3, which, coupled[which])
            else:
                height[which, PAD : PAD + LAT, :] = new_h[which]
                tracer[which, PAD : PAD + LAT, :] = coupled[which]


def exchange(upper, lower, both_wet):
    return jnp.where(both_wet, vertical_mix * (lower - upper), 0.0)


def couple_levels(moved, wets):
    swaps = [exchange(moved[k], moved[k + 1], wets[k] & wets[k + 1]) for k in range(LEV - 1)]
    return [
        moved[0] + swaps[0],
        moved[1] + swaps[1] - swaps[0],
        moved[2] + swaps[2] - swaps[1],
        moved[3] - swaps[2],
    ]


def couple_pairs(moved, wets):
    even, odd = moved
    within = exchange(even, odd, wets[0] & wets[1])
    lane = lanes_of(LAT)
    wet_even = jnp.where(wets[0], 1.0, 0.0)
    turned = pltpu.roll(even, TILE, 1)
    turned_wet = pltpu.roll(wet_even, TILE, 1) > 0.0
    between = exchange(odd, turned, wets[1] & turned_wet & (lane < TILE))
    return [even + within - pltpu.roll(between, TILE, 1), odd + between - within]


def scratch_for(count):
    return [pltpu.VMEM((count, LAT + 2 * PAD, WIDTH), jnp.float32)] * 8


STRIP = 2 * HALO
PROWS = 128


def inner_kernel(fields_ref, depth_ref, levels_ref, out_ref, strip_ref, *scratch):
    lane = lanes_of(LAT)
    for kind, level, slot, half in groups():
        values = values_of(fields_ref, depth_ref, levels_ref, kind, level, 0, LAT)
        scratch[kind][level, PAD : PAD + LAT, :] = values
        base = half * TILE
        ends = jnp.where(
            lane < base + 24, pltpu.roll(values, base + STRIP, 1), pltpu.roll(values, base + 2 * STRIP, 1)
        )
        if half:
            strip_ref[slot] = jnp.where(lane < TILE, strip_ref[slot], ends)
        else:
            strip_ref[slot] = ends

    def emit(kind, level, values):
        out_ref[kind * LEV + level] = values

    march(scratch, LEV, couple_levels, emit)


def run_inner(fields, depth, levels):
    return pl.pallas_call(
        inner_kernel,
        out_shape=(
            jax.ShapeDtypeStruct(fields.shape, fields.dtype),
            jax.ShapeDtypeStruct((2 * (FIELDS + 1), LAT, WIDTH), fields.dtype),
        ),
        in_specs=vmem(3),
        out_specs=tuple(vmem(2)),
        scratch_shapes=scratch_for(LEV),
        compiler_params=pltpu.CompilerParams(vmem_limit_bytes=VMEM_LIMIT),
        cost_estimate=pl.CostEstimate(flops=75 * fields.size, bytes_accessed=12 * fields.size, transcendentals=0),
        name="inner",
    )(fields, depth, levels)


def ends_kernel(inner_ref, strip_ref, before_ref, after_ref, out_ref, result_ref, sems, *scratch):
    lane = lanes_of(LAT)
    place = lane % TILE
    in_after = (place >= STRIP) & (place < STRIP + HALO)
    in_before = (place >= STRIP + HALO) & (place < 2 * STRIP)
    before = before_ref[...]
    after = after_ref[...]
    for kind in range(FIELDS + 1):
        for which in range(2):
            slot = kind * 2 + which
            low = HALO * slot
            values = jnp.where(
                in_after,
                pltpu.roll(after, (WIDTH + STRIP - low - HALO) % WIDTH, 1),
                jnp.where(
                    in_before, pltpu.roll(before, (WIDTH + STRIP + HALO - low) % WIDTH, 1), strip_ref[slot]
                ),
            )
            scratch[kind][which, PAD : PAD + LAT, :] = values

    def emit(kind, which, values):
        for half in range(2):
            base = half * TILE
            at = kind * LEV + which + 2 * half
            last_columns = pltpu.roll(values, (WIDTH - STRIP - base) % WIDTH, 1)
            first_columns = pltpu.roll(values, (2 * WIDTH - base - 2 * STRIP) % WIDTH, 1)
            result_ref[at] = jnp.where(
                lane < HALO, first_columns, jnp.where(lane >= WIDTH - HALO, last_columns, inner_ref[at])
            )

    copies = [
        pltpu.make_async_copy(
            result_ref.at[kind * LEV : kind * LEV + LEV], out_ref.at[kind * LEV : kind * LEV + LEV], sems.at[kind]
        )
        for kind in range(FIELDS)
    ]

    def winds_done():
        copies[1].start()
        copies[2].start()

    march(scratch, 2, couple_pairs, emit, winds_done)
    copies[0].start()
    copies[3].start()
    for copy in copies:
        copy.wait()


def run_ends(inner, strips, before, after):
    return pl.pallas_call(
        ends_kernel,
        out_shape=jax.ShapeDtypeStruct(inner.shape, inner.dtype),
        in_specs=vmem(4),
        out_specs=pl.BlockSpec(memory_space=pl.ANY),
        scratch_shapes=[pltpu.VMEM(inner.shape, inner.dtype), pltpu.SemaphoreType.DMA((FIELDS,))] + scratch_for(2),
        compiler_params=pltpu.CompilerParams(vmem_limit_bytes=VMEM_LIMIT),
        cost_estimate=pl.CostEstimate(flops=40 * inner.size, bytes_accessed=12 * inner.size, transcendentals=0),
        name="ends",
    )(inner, strips, before, after)


def run_forecast(fields, depth, levels, before, after):
    inner, strips = run_inner(fields, depth, levels)
    return run_ends(inner, strips, before, after)


def ring(values, axis, shift):
    size = lax.axis_size(axis)
    return lax.ppermute(values, axis, [(i, (i + shift) % size) for i in range(size)])


def take_turns(values):
    bands = lax.axis_size("lon")
    halves, columns, layers = DOM
    pairs = []
    for here in range(halves * columns * layers):
        half, column, layer = here // (columns * layers), here // layers % columns, here % layers
        there = (half + HOP[0]) % halves
        there = there * columns + (column + HOP[1]) % columns
        there = there * layers + (layer + HOP[2]) % layers
        pairs += [(here * bands + band, there * bands + band) for band in range(1, bands, 2)]
    return lax.ppermute(values, ("dom", "lon"), pairs)


def on_device(state, level_thickness, wet_levels, ancestors):
    size = lax.axis_size("dom")
    own = ancestors.reshape(1, -1)
    left = ring(own, "lon", 1)
    right = ring(own, "lon", -1)
    chunks = make_chunks(state.reshape(size, -1, WIDTH))
    left, right = lax.optimization_barrier((left, right))
    chunks = add_table(chunks, own, left, right, take_turns(left), size)
    sent = chunks.reshape(size, -1, 1, WIDTH)
    block = lax.all_to_all(sent, "dom", split_axis=0, concat_axis=0, tiled=True)
    mixed = blend(block.reshape(chunks.shape), size)
    back = lax.all_to_all(mixed, "dom", split_axis=0, concat_axis=0, tiled=True)
    fields = back.reshape(FIELDS * LEV, LAT, WIDTH)
    right, left = pack(fields, level_thickness, wet_levels)
    before = ring(right, "lon", 1)
    after = ring(left, "lon", -1)
    result = run_forecast(fields, level_thickness, wet_levels, before, after)
    return result.reshape(state.shape)


def solution(mesh):
    return jax.shard_map(
        on_device,
        mesh=mesh,
        in_specs=(
            P("dom", None, None, None, "lon"),
            P(None, None, "lon"),
            P(None, "lon"),
            P("dom", "lon", None),
        ),
        out_specs=P("dom", None, None, None, "lon"),
        check_vma=False,
    )
```

```python
import jax
import jax.numpy as jnp
from jax import lax
from jax.experimental import pallas as pl
from jax.experimental.pallas import tpu as pltpu
from jax.sharding import PartitionSpec as P

LEV = 4
FIELDS = 4
TILE = 64
BLEND = 8
STEPS = 3
LAT = 128
WIDTH = 128
HALO = 2 * STEPS
PAIRS = ((0, 3), (1, 2))
DOM = (2, 4, 8)
HOP = (1, 2, 4)
PAD = 8

time_step = 0.3
gravity = 1.0
drag_rate = 0.05
diffusion = 0.1
vertical_mix = 0.2
coriolis_base = 0.1
coriolis_slope = 0.3

VMEM_LIMIT = 16 * 1024 * 1024


def lanes_of(rows):
    return lax.broadcasted_iota(jnp.int32, (rows, WIDTH), 1)


def vmem(count):
    return [pl.BlockSpec(memory_space=pltpu.VMEM)] * count


def chunk_kernel(state_ref, out_ref):
    height = state_ref.shape[1]
    for chunk in range(state_ref.shape[0]):
        base = chunk * (height + 1)
        out_ref[base : base + height, :] = state_ref[chunk]


def make_chunks(chunks):
    count, height, width = chunks.shape
    shape = (count * (height + 1), width)
    return pl.pallas_call(
        chunk_kernel,
        out_shape=jax.ShapeDtypeStruct(shape, chunks.dtype),
        in_specs=vmem(1),
        out_specs=pl.BlockSpec(memory_space=pltpu.VMEM),
        compiler_params=pltpu.CompilerParams(vmem_limit_bytes=VMEM_LIMIT),
        cost_estimate=pl.CostEstimate(flops=0, bytes_accessed=8 * chunks.size, transcendentals=0),
        name="chunks",
    )(chunks)


def add_table(chunks, own, left, right, turn, count):
    height = chunks.shape[0] // count

    def table_kernel(own_ref, left_ref, right_ref, turn_ref, chunks_ref, out_ref):
        del turn_ref, chunks_ref
        tile = lanes_of(1) % 4
        picks = (left_ref[0:1, 1:2], own_ref[0:1, 0:1], own_ref[0:1, 1:2], right_ref[0:1, 0:1])
        row = jnp.zeros((1, WIDTH), jnp.int32)
        for at, pick in enumerate(picks):
            row = jnp.where(tile == at, pick, row)
        row = row.astype(jnp.float32)
        for chunk in range(count):
            base = chunk * height + height - 1
            out_ref[base : base + 1, :] = row

    return pl.pallas_call(
        table_kernel,
        out_shape=jax.ShapeDtypeStruct(chunks.shape, chunks.dtype),
        in_specs=vmem(5),
        out_specs=pl.BlockSpec(memory_space=pltpu.VMEM),
        input_output_aliases={4: 0},
        compiler_params=pltpu.CompilerParams(vmem_limit_bytes=VMEM_LIMIT),
        cost_estimate=pl.CostEstimate(flops=0, bytes_accessed=4 * count * WIDTH, transcendentals=0),
        name="table",
    )(own, left, right, turn, chunks)


SHARE = WIDTH // 4
TOGETHER = 8
BROWS = 32
UNROLL = 2


def blend_kernel(block_ref, out_ref, numbers_ref, table_ref, sem):
    particles, rows, _ = out_ref.shape
    table = block_ref[pl.ds(rows, particles, stride=rows + 1), :]
    holder = lax.broadcasted_iota(jnp.int32, (particles, WIDTH), 0) % SHARE
    table = jnp.where(lanes_of(particles) // 4 == holder, table, 0.0)
    for line in range(particles // SHARE):
        total = jnp.sum(table[line * SHARE : (line + 1) * SHARE], axis=0, keepdims=True)
        numbers_ref[line : line + 1, :] = total.astype(jnp.int32)
    copy = pltpu.make_async_copy(numbers_ref, table_ref, sem)
    copy.start()
    lane = lanes_of(BROWS)
    position = lane % TILE
    near_left = position < BLEND
    near_right = position >= TILE - BLEND
    distance = jnp.where(near_left, position, TILE - 1 - position).astype(jnp.float32)
    weight = jnp.where(near_left | near_right, 0.5 + (distance + 0.5) / (2.0 * BLEND), 1.0)
    rest = 1.0 - weight
    first = lane < TILE
    zero = jnp.zeros_like(weight)
    weights = (
        jnp.where(first & near_left, rest, zero),
        jnp.where(first, weight, jnp.where(near_left, rest, zero)),
        jnp.where(first, jnp.where(near_right, rest, zero), weight),
        jnp.where(first, zero, jnp.where(near_right, rest, zero)),
    )
    copy.wait()

    def some(at, carry):
        done = []
        for particle in range(TOGETHER):
            particle = at * TOGETHER + particle
            line, first_tile = particle // SHARE, 4 * (particle % SHARE)
            picks = [table_ref[line, first_tile + tile] * (rows + 1) for tile in range(4)]
            for row in range(0, rows, BROWS):
                parts = [block_ref[pl.ds(pick + row, BROWS), :] * w for pick, w in zip(picks, weights)]
                done.append((particle, row, (parts[1] + parts[2]) + (parts[0] + parts[3])))
        for particle, row, values in done:
            out_ref[particle, row : row + BROWS, :] = values
        return carry

    lax.fori_loop(0, particles // TOGETHER, some, 0, unroll=UNROLL)


def blend(block, particles):
    rows = block.shape[0] // particles - 1
    shape = (particles, rows, WIDTH)
    return pl.pallas_call(
        blend_kernel,
        out_shape=jax.ShapeDtypeStruct(shape, block.dtype),
        in_specs=vmem(1),
        out_specs=pl.BlockSpec(memory_space=pltpu.VMEM),
        scratch_shapes=[
            pltpu.VMEM((particles // SHARE, WIDTH), jnp.int32),
            pltpu.SMEM((particles // SHARE, WIDTH), jnp.int32),
            pltpu.SemaphoreType.DMA,
        ],
        compiler_params=pltpu.CompilerParams(vmem_limit_bytes=VMEM_LIMIT),
        cost_estimate=pl.CostEstimate(flops=4 * block.size, bytes_accessed=8 * block.size, transcendentals=0),
        name="blend",
    )(block)


def masked_thickness(depth_ref, levels_ref, level, start, rows):
    wet = levels_ref[pl.ds(start, rows), :] > level
    return jnp.where(wet, depth_ref[level, pl.ds(start, rows), :], 0.0)


def groups():
    for kind in range(FIELDS + 1):
        for which, pair in enumerate(PAIRS):
            for half, level in enumerate(pair):
                yield kind, level, kind * 2 + which, half


def values_of(fields_ref, depth_ref, levels_ref, kind, level, start, rows):
    if kind < FIELDS:
        return fields_ref[kind * LEV + level, pl.ds(start, rows), :]
    return masked_thickness(depth_ref, levels_ref, level, start, rows)


def pack_kernel(fields_ref, depth_ref, levels_ref, right_ref, left_ref):
    lane = lanes_of(PROWS)

    def within(low):
        return ((lane + (WIDTH - low)) % WIDTH) < HALO

    for start in range(0, LAT, PROWS):
        right = jnp.zeros((PROWS, WIDTH), jnp.float32)
        left = jnp.zeros((PROWS, WIDTH), jnp.float32)
        for kind, level, slot, half in groups():
            values = values_of(fields_ref, depth_ref, levels_ref, kind, level, start, PROWS)
            low = half * TILE + HALO * slot
            turned = pltpu.roll(values, (low + HALO) % WIDTH, 1)
            right = jnp.where(within(low), turned, right)
            left = jnp.where(within(low + HALO), turned, left)
        right_ref[start : start + PROWS, :] = right
        left_ref[start : start + PROWS, :] = left


def pack(fields, depth, levels):
    shape = jax.ShapeDtypeStruct((LAT, WIDTH), jnp.float32)
    return pl.pallas_call(
        pack_kernel,
        out_shape=(shape, shape),
        in_specs=vmem(3),
        out_specs=tuple(vmem(2)),
        compiler_params=pltpu.CompilerParams(vmem_limit_bytes=VMEM_LIMIT),
        cost_estimate=pl.CostEstimate(flops=4 * fields.size, bytes_accessed=5 * fields.size, transcendentals=0),
        name="pack",
    )(fields, depth, levels)


def march(scratch, count, couple, emit, winds_done=lambda: None):
    height, zonal, merid, tracer, thick, flux, south, north = scratch

    def rows_at(ref, shift):
        return ref[:, PAD + shift : PAD + LAT + shift, :]

    def put(ref, values):
        ref[:, PAD : PAD + LAT, :] = values

    def east(values):
        return pltpu.roll(values, WIDTH - 1, 2)

    def west(values):
        return pltpu.roll(values, 1, 2)

    edge = jnp.zeros((count, PAD, WIDTH), jnp.float32)
    for ref in (height, flux, south, north):
        ref[:, 0:PAD, :] = edge
        ref[:, PAD + LAT : 2 * PAD + LAT, :] = edge

    half = 0.5 * time_step
    keep = 1.0 - time_step * drag_rate
    row = lax.broadcasted_iota(jnp.int32, (LAT, WIDTH), 0)
    turn = time_step * (coriolis_base + coriolis_slope * row.astype(jnp.float32) / LAT)
    turn = turn[None]

    for step in range(STEPS):
        last = step == STEPS - 1
        h, u, v, c, t = (rows_at(ref, 0) for ref in (height, zonal, merid, tracer, thick))
        wet = t > 0.0
        dx = east(h) - west(h)
        dy = rows_at(height, 1) - rows_at(height, -1)
        new_u = jnp.where(wet, keep * u + turn * v - (half * gravity) * dx, 0.0)
        new_v = jnp.where(wet, keep * v - turn * u - (half * gravity) * dy, 0.0)
        some, more = diffusion * c, half * c
        along, cross = more * new_u, more * new_v
        across = t * new_u
        put(flux, t * new_v)
        put(south, some - cross)
        put(north, some + cross)
        if last:
            for which in range(count):
                emit(1, which, new_u[which])
                emit(2, which, new_v[which])
            winds_done()
        else:
            put(zonal, new_u)
            put(merid, new_v)
        part = h - half * (east(across) - west(across))
        c_part = (1.0 - 4.0 * diffusion) * c + (east(some - along) + west(some + along))
        dy = rows_at(flux, 1) - rows_at(flux, -1)
        new_h = jnp.where(wet, part - half * dy, 0.0)
        new_c = jnp.where(wet, c_part + (rows_at(south, 1) + rows_at(north, -1)), 0.0)
        moved = [new_c[which] for which in range(count)]
        wets = [wet[which] for which in range(count)]
        coupled = couple(moved, wets)
        for which in range(count):
            if last:
                emit(0, which, new_h[which])
                emit(3, which, coupled[which])
            else:
                height[which, PAD : PAD + LAT, :] = new_h[which]
                tracer[which, PAD : PAD + LAT, :] = coupled[which]


def exchange(upper, lower, both_wet):
    return jnp.where(both_wet, vertical_mix * (lower - upper), 0.0)


def couple_levels(moved, wets):
    swaps = [exchange(moved[k], moved[k + 1], wets[k] & wets[k + 1]) for k in range(LEV - 1)]
    return [
        moved[0] + swaps[0],
        moved[1] + swaps[1] - swaps[0],
        moved[2] + swaps[2] - swaps[1],
        moved[3] - swaps[2],
    ]


def couple_pairs():
    known = []

    def couple(moved, wets):
        outer, middle = moved
        if not known:
            turned_wet = pltpu.roll(jnp.where(wets[1], 1.0, 0.0), TILE, 1) > 0.0
            known.append(jnp.where(wets[1] & turned_wet, vertical_mix, 0.0))
        across = exchange(outer, middle, wets[0] & wets[1])
        between = known[0] * (pltpu.roll(middle, TILE, 1) - middle)
        return [outer + across, middle + between - across]

    return couple


def scratch_for(count):
    return [pltpu.VMEM((count, LAT + 2 * PAD, WIDTH), jnp.float32)] * 8


STRIP = 2 * HALO
PROWS = 128


def ring_base(half):
    return (WIDTH - STRIP + TILE * half) % WIDTH


def turned(values, shift):
    return pltpu.roll(values, shift % WIDTH, 1) if shift % WIDTH else values


def inner_kernel(fields_ref, depth_ref, levels_ref, out_ref, strip_ref, *scratch):
    lane = lanes_of(LAT)
    place = (lane + (WIDTH - ring_base(0))) % TILE
    second = (lane >= ring_base(1)) & (lane < ring_base(0))
    for kind, level, slot, half in groups():
        values = values_of(fields_ref, depth_ref, levels_ref, kind, level, 0, LAT)
        scratch[kind][level, PAD : PAD + LAT, :] = values
        base = ring_base(half)
        ends = jnp.where(
            place < 2 * STRIP, turned(values, base - (WIDTH - STRIP)), turned(values, base + 2 * STRIP)
        )
        if half:
            strip_ref[slot] = jnp.where(second, ends, strip_ref[slot])
        else:
            strip_ref[slot] = ends

    def emit(kind, level, values):
        out_ref[kind * LEV + level] = values

    march(scratch, LEV, couple_levels, emit)


def run_inner(fields, depth, levels):
    return pl.pallas_call(
        inner_kernel,
        out_shape=(
            jax.ShapeDtypeStruct(fields.shape, fields.dtype),
            jax.ShapeDtypeStruct((2 * (FIELDS + 1), LAT, WIDTH), fields.dtype),
        ),
        in_specs=vmem(3),
        out_specs=tuple(vmem(2)),
        scratch_shapes=scratch_for(LEV),
        compiler_params=pltpu.CompilerParams(vmem_limit_bytes=VMEM_LIMIT),
        cost_estimate=pl.CostEstimate(flops=75 * fields.size, bytes_accessed=12 * fields.size, transcendentals=0),
        name="inner",
    )(fields, depth, levels)


def ends_kernel(inner_ref, strip_ref, before_ref, after_ref, out_ref, result_ref, sems, *scratch):
    lane = lanes_of(LAT)
    place = (lane + (WIDTH - ring_base(0))) % TILE
    in_after = (place >= STRIP) & (place < STRIP + HALO)
    in_before = (place >= STRIP + HALO) & (place < 2 * STRIP)
    before = before_ref[...]
    after = after_ref[...]
    for kind in range(FIELDS + 1):
        for which in range(2):
            slot = kind * 2 + which
            low = HALO * slot
            values = jnp.where(
                in_after,
                turned(after, ring_base(0) + STRIP - low - HALO),
                jnp.where(
                    in_before, turned(before, ring_base(0) + STRIP + HALO - low), strip_ref[slot]
                ),
            )
            scratch[kind][which, PAD : PAD + LAT, :] = values

    def emit(kind, which, values):
        for half in range(2):
            base = ring_base(half)
            at = kind * LEV + PAIRS[which][half]
            last_columns = turned(values, WIDTH - STRIP - base)
            first_columns = turned(values, -(base + 2 * STRIP))
            result_ref[at] = jnp.where(
                lane < HALO, first_columns, jnp.where(lane >= WIDTH - HALO, last_columns, inner_ref[at])
            )

    copies = [
        pltpu.make_async_copy(
            result_ref.at[kind * LEV : kind * LEV + LEV], out_ref.at[kind * LEV : kind * LEV + LEV], sems.at[kind]
        )
        for kind in range(FIELDS)
    ]

    def winds_done():
        copies[1].start()
        copies[2].start()

    march(scratch, 2, couple_pairs(), emit, winds_done)
    copies[0].start()
    copies[3].start()
    for copy in copies:
        copy.wait()


def run_ends(inner, strips, before, after):
    return pl.pallas_call(
        ends_kernel,
        out_shape=jax.ShapeDtypeStruct(inner.shape, inner.dtype),
        in_specs=vmem(4),
        out_specs=pl.BlockSpec(memory_space=pl.ANY),
        scratch_shapes=[pltpu.VMEM(inner.shape, inner.dtype), pltpu.SemaphoreType.DMA((FIELDS,))] + scratch_for(2),
        compiler_params=pltpu.CompilerParams(vmem_limit_bytes=VMEM_LIMIT),
        cost_estimate=pl.CostEstimate(flops=40 * inner.size, bytes_accessed=12 * inner.size, transcendentals=0),
        name="ends",
    )(inner, strips, before, after)


def run_forecast(fields, depth, levels, before, after):
    inner, strips = run_inner(fields, depth, levels)
    return run_ends(inner, strips, before, after)


def ring(values, axis, shift):
    size = lax.axis_size(axis)
    return lax.ppermute(values, axis, [(i, (i + shift) % size) for i in range(size)])


def take_turns(values):
    bands = lax.axis_size("lon")
    halves, columns, layers = DOM
    pairs = []
    for here in range(halves * columns * layers):
        half, column, layer = here // (columns * layers), here // layers % columns, here % layers
        there = (half + HOP[0]) % halves
        there = there * columns + (column + HOP[1]) % columns
        there = there * layers + (layer + HOP[2]) % layers
        pairs += [(here * bands + band, there * bands + band) for band in range(1, bands, 2)]
    return lax.ppermute(values, ("dom", "lon"), pairs)


def on_device(state, level_thickness, wet_levels, ancestors):
    size = lax.axis_size("dom")
    own = ancestors.reshape(1, -1)
    left = ring(own, "lon", 1)
    right = ring(own, "lon", -1)
    chunks = make_chunks(state.reshape(size, -1, WIDTH))
    left, right = lax.optimization_barrier((left, right))
    chunks = add_table(chunks, own, left, right, take_turns(left), size)
    sent = chunks.reshape(size, -1, 1, WIDTH)
    block = lax.all_to_all(sent, "dom", split_axis=0, concat_axis=0, tiled=True)
    mixed = blend(block.reshape(chunks.shape), size)
    back = lax.all_to_all(mixed, "dom", split_axis=0, concat_axis=0, tiled=True)
    fields = back.reshape(FIELDS * LEV, LAT, WIDTH)
    right, left = pack(fields, level_thickness, wet_levels)
    before = ring(right, "lon", 1)
    after = ring(left, "lon", -1)
    result = run_forecast(fields, level_thickness, wet_levels, before, after)
    return result.reshape(state.shape)


def solution(mesh):
    return jax.shard_map(
        on_device,
        mesh=mesh,
        in_specs=(
            P("dom", None, None, None, "lon"),
            P(None, None, "lon"),
            P(None, "lon"),
            P("dom", "lon", None),
        ),
        out_specs=P("dom", None, None, None, "lon"),
        check_vma=False,
    )
```

```python
import jax
import jax.numpy as jnp
from jax import lax
from jax.experimental import pallas as pl
from jax.experimental.pallas import tpu as pltpu
from jax.sharding import PartitionSpec as P

LEV = 4
FIELDS = 4
TILE = 64
BLEND = 8
STEPS = 3
LAT = 128
WIDTH = 128
HALO = 2 * STEPS
PAIRS = ((0, 3), (1, 2))
DOM = (2, 4, 8)
HOP = (1, 2, 4)
PAD = 8

time_step = 0.3
gravity = 1.0
drag_rate = 0.05
diffusion = 0.1
vertical_mix = 0.2
coriolis_base = 0.1
coriolis_slope = 0.3

VMEM_LIMIT = 16 * 1024 * 1024


def lanes_of(rows):
    return lax.broadcasted_iota(jnp.int32, (rows, WIDTH), 1)


def vmem(count):
    return [pl.BlockSpec(memory_space=pltpu.VMEM)] * count


def chunk_kernel(state_ref, out_ref):
    height = state_ref.shape[1]
    for chunk in range(state_ref.shape[0]):
        base = chunk * (height + 1)
        out_ref[base : base + height, :] = state_ref[chunk]


def make_chunks(chunks):
    count, height, width = chunks.shape
    shape = (count * (height + 1), width)
    return pl.pallas_call(
        chunk_kernel,
        out_shape=jax.ShapeDtypeStruct(shape, chunks.dtype),
        in_specs=vmem(1),
        out_specs=pl.BlockSpec(memory_space=pltpu.VMEM),
        compiler_params=pltpu.CompilerParams(vmem_limit_bytes=VMEM_LIMIT),
        cost_estimate=pl.CostEstimate(flops=0, bytes_accessed=8 * chunks.size, transcendentals=0),
        name="chunks",
    )(chunks)


def add_table(chunks, own, left, right, turn, count):
    height = chunks.shape[0] // count

    def table_kernel(own_ref, left_ref, right_ref, turn_ref, chunks_ref, out_ref):
        del turn_ref, chunks_ref
        tile = lanes_of(1) % 4
        picks = (left_ref[0:1, 1:2], own_ref[0:1, 0:1], own_ref[0:1, 1:2], right_ref[0:1, 0:1])
        row = jnp.zeros((1, WIDTH), jnp.int32)
        for at, pick in enumerate(picks):
            row = jnp.where(tile == at, pick, row)
        row = row.astype(jnp.float32)
        for chunk in range(count):
            base = chunk * height + height - 1
            out_ref[base : base + 1, :] = row

    return pl.pallas_call(
        table_kernel,
        out_shape=jax.ShapeDtypeStruct(chunks.shape, chunks.dtype),
        in_specs=vmem(5),
        out_specs=pl.BlockSpec(memory_space=pltpu.VMEM),
        input_output_aliases={4: 0},
        compiler_params=pltpu.CompilerParams(vmem_limit_bytes=VMEM_LIMIT),
        cost_estimate=pl.CostEstimate(flops=0, bytes_accessed=4 * count * WIDTH, transcendentals=0),
        name="table",
    )(own, left, right, turn, chunks)


SHARE = WIDTH // 4
TOGETHER = 8
BROWS = 32
UNROLL = 8


def blend_kernel(block_ref, out_ref, numbers_ref, table_ref, sem):
    particles, rows, _ = out_ref.shape
    table = block_ref[pl.ds(rows, particles, stride=rows + 1), :]
    holder = lax.broadcasted_iota(jnp.int32, (particles, WIDTH), 0) % SHARE
    table = jnp.where(lanes_of(particles) // 4 == holder, table, 0.0)
    for line in range(particles // SHARE):
        total = jnp.sum(table[line * SHARE : (line + 1) * SHARE], axis=0, keepdims=True)
        numbers_ref[line : line + 1, :] = total.astype(jnp.int32)
    copy = pltpu.make_async_copy(numbers_ref, table_ref, sem)
    copy.start()
    lane = lanes_of(BROWS)
    position = lane % TILE
    near_left = position < BLEND
    near_right = position >= TILE - BLEND
    distance = jnp.where(near_left, position, TILE - 1 - position).astype(jnp.float32)
    weight = jnp.where(near_left | near_right, 0.5 + (distance + 0.5) / (2.0 * BLEND), 1.0)
    rest = 1.0 - weight
    first = lane < TILE
    zero = jnp.zeros_like(weight)
    weights = (
        jnp.where(first & near_left, rest, zero),
        jnp.where(first, weight, jnp.where(near_left, rest, zero)),
        jnp.where(first, jnp.where(near_right, rest, zero), weight),
        jnp.where(first, zero, jnp.where(near_right, rest, zero)),
    )
    copy.wait()

    def some(at, carry):
        done = []
        for particle in range(TOGETHER):
            particle = at * TOGETHER + particle
            line, first_tile = particle // SHARE, 4 * (particle % SHARE)
            picks = [table_ref[line, first_tile + tile] * (rows + 1) for tile in range(4)]
            for row in range(0, rows, BROWS):
                parts = [block_ref[pl.ds(pick + row, BROWS), :] * w for pick, w in zip(picks, weights)]
                done.append((particle, row, (parts[1] + parts[2]) + (parts[0] + parts[3])))
        for particle, row, values in done:
            out_ref[particle, row : row + BROWS, :] = values
        return carry

    lax.fori_loop(0, particles // TOGETHER, some, 0, unroll=UNROLL)


def blend(block, particles):
    rows = block.shape[0] // particles - 1
    shape = (particles, rows, WIDTH)
    return pl.pallas_call(
        blend_kernel,
        out_shape=jax.ShapeDtypeStruct(shape, block.dtype),
        in_specs=vmem(1),
        out_specs=pl.BlockSpec(memory_space=pltpu.VMEM),
        scratch_shapes=[
            pltpu.VMEM((particles // SHARE, WIDTH), jnp.int32),
            pltpu.SMEM((particles // SHARE, WIDTH), jnp.int32),
            pltpu.SemaphoreType.DMA,
        ],
        compiler_params=pltpu.CompilerParams(vmem_limit_bytes=VMEM_LIMIT),
        cost_estimate=pl.CostEstimate(flops=4 * block.size, bytes_accessed=8 * block.size, transcendentals=0),
        name="blend",
    )(block)


def masked_thickness(depth_ref, levels_ref, level, start, rows):
    wet = levels_ref[pl.ds(start, rows), :] > level
    return jnp.where(wet, depth_ref[level, pl.ds(start, rows), :], 0.0)


def groups():
    for kind in range(FIELDS + 1):
        for which, pair in enumerate(PAIRS):
            for half, level in enumerate(pair):
                yield kind, level, kind * 2 + which, half


def values_of(fields_ref, depth_ref, levels_ref, kind, level, start, rows):
    if kind < FIELDS:
        return fields_ref[kind * LEV + level, pl.ds(start, rows), :]
    return masked_thickness(depth_ref, levels_ref, level, start, rows)


def pack_kernel(fields_ref, depth_ref, levels_ref, right_ref, left_ref):
    lane = lanes_of(PROWS)

    def within(low):
        return ((lane + (WIDTH - low)) % WIDTH) < HALO

    for start in range(0, LAT, PROWS):
        right = jnp.zeros((PROWS, WIDTH), jnp.float32)
        left = jnp.zeros((PROWS, WIDTH), jnp.float32)
        for kind, level, slot, half in groups():
            values = values_of(fields_ref, depth_ref, levels_ref, kind, level, start, PROWS)
            low = half * TILE + HALO * slot
            turned = pltpu.roll(values, (low + HALO) % WIDTH, 1)
            right = jnp.where(within(low), turned, right)
            left = jnp.where(within(low + HALO), turned, left)
        right_ref[start : start + PROWS, :] = right
        left_ref[start : start + PROWS, :] = left


def pack(fields, depth, levels):
    shape = jax.ShapeDtypeStruct((LAT, WIDTH), jnp.float32)
    return pl.pallas_call(
        pack_kernel,
        out_shape=(shape, shape),
        in_specs=vmem(3),
        out_specs=tuple(vmem(2)),
        compiler_params=pltpu.CompilerParams(vmem_limit_bytes=VMEM_LIMIT),
        cost_estimate=pl.CostEstimate(flops=4 * fields.size, bytes_accessed=5 * fields.size, transcendentals=0),
        name="pack",
    )(fields, depth, levels)


def march(scratch, count, couple, emit):
    height, zonal, merid, tracer, thick, flux, south, north = scratch

    def rows_at(ref, shift):
        return ref[:, PAD + shift : PAD + LAT + shift, :]

    def put(ref, values):
        ref[:, PAD : PAD + LAT, :] = values

    def east(values):
        return pltpu.roll(values, WIDTH - 1, 2)

    def west(values):
        return pltpu.roll(values, 1, 2)

    edge = jnp.zeros((count, PAD, WIDTH), jnp.float32)
    for ref in (height, flux, south, north):
        ref[:, 0:PAD, :] = edge
        ref[:, PAD + LAT : 2 * PAD + LAT, :] = edge

    half = 0.5 * time_step
    keep = 1.0 - time_step * drag_rate
    row = lax.broadcasted_iota(jnp.int32, (LAT, WIDTH), 0)
    turn = time_step * (coriolis_base + coriolis_slope * row.astype(jnp.float32) / LAT)
    turn = turn[None]

    for step in range(STEPS):
        last = step == STEPS - 1
        h, u, v, c, t = (rows_at(ref, 0) for ref in (height, zonal, merid, tracer, thick))
        wet = t > 0.0
        dx = east(h) - west(h)
        dy = rows_at(height, 1) - rows_at(height, -1)
        new_u = jnp.where(wet, keep * u + turn * v - (half * gravity) * dx, 0.0)
        new_v = jnp.where(wet, keep * v - turn * u - (half * gravity) * dy, 0.0)
        some, more = diffusion * c, half * c
        along, cross = more * new_u, more * new_v
        across = t * new_u
        put(flux, t * new_v)
        put(south, some - cross)
        put(north, some + cross)
        if last:
            for which in range(count):
                emit(1, which, new_u[which])
                emit(2, which, new_v[which])
        else:
            put(zonal, new_u)
            put(merid, new_v)
        part = h - half * (east(across) - west(across))
        c_part = (1.0 - 4.0 * diffusion) * c + (east(some - along) + west(some + along))
        dy = rows_at(flux, 1) - rows_at(flux, -1)
        new_h = jnp.where(wet, part - half * dy, 0.0)
        new_c = jnp.where(wet, c_part + (rows_at(south, 1) + rows_at(north, -1)), 0.0)
        if last:
            for which in range(count):
                emit(0, which, new_h[which])
        moved = [new_c[which] for which in range(count)]
        wets = [wet[which] for which in range(count)]
        coupled = couple(moved, wets)
        for which in range(count):
            if last:
                emit(3, which, coupled[which])
            else:
                height[which, PAD : PAD + LAT, :] = new_h[which]
                tracer[which, PAD : PAD + LAT, :] = coupled[which]


def exchange(upper, lower, both_wet):
    return jnp.where(both_wet, vertical_mix * (lower - upper), 0.0)


def couple_levels(moved, wets):
    swaps = [exchange(moved[k], moved[k + 1], wets[k] & wets[k + 1]) for k in range(LEV - 1)]
    return [
        moved[0] + swaps[0],
        moved[1] + swaps[1] - swaps[0],
        moved[2] + swaps[2] - swaps[1],
        moved[3] - swaps[2],
    ]


def couple_pairs():
    known = []

    def couple(moved, wets):
        outer, middle = moved
        if not known:
            turned_wet = pltpu.roll(jnp.where(wets[1], 1.0, 0.0), TILE, 1) > 0.0
            known.append(jnp.where(wets[1] & turned_wet, vertical_mix, 0.0))
        across = exchange(outer, middle, wets[0] & wets[1])
        between = known[0] * (pltpu.roll(middle, TILE, 1) - middle)
        return [outer + across, middle + between - across]

    return couple


def scratch_for(count):
    return [pltpu.VMEM((count, LAT + 2 * PAD, WIDTH), jnp.float32)] * 8


STRIP = 2 * HALO
PROWS = 128


def ring_base(half):
    return (WIDTH - STRIP + TILE * half) % WIDTH


def turned(values, shift):
    return pltpu.roll(values, shift % WIDTH, 1) if shift % WIDTH else values


def inner_kernel(fields_ref, depth_ref, levels_ref, out_ref, strip_ref, *scratch):
    lane = lanes_of(LAT)
    place = (lane + (WIDTH - ring_base(0))) % TILE
    second = (lane >= ring_base(1)) & (lane < ring_base(0))
    for kind, level, slot, half in groups():
        values = values_of(fields_ref, depth_ref, levels_ref, kind, level, 0, LAT)
        scratch[kind][level, PAD : PAD + LAT, :] = values
        base = ring_base(half)
        ends = jnp.where(
            place < 2 * STRIP, turned(values, base - (WIDTH - STRIP)), turned(values, base + 2 * STRIP)
        )
        if half:
            strip_ref[slot] = jnp.where(second, ends, strip_ref[slot])
        else:
            strip_ref[slot] = ends

    def emit(kind, level, values):
        out_ref[kind * LEV + level] = values

    march(scratch, LEV, couple_levels, emit)


def run_inner(fields, depth, levels):
    return pl.pallas_call(
        inner_kernel,
        out_shape=(
            jax.ShapeDtypeStruct(fields.shape, fields.dtype),
            jax.ShapeDtypeStruct((2 * (FIELDS + 1), LAT, WIDTH), fields.dtype),
        ),
        in_specs=vmem(3),
        out_specs=tuple(vmem(2)),
        scratch_shapes=scratch_for(LEV),
        compiler_params=pltpu.CompilerParams(vmem_limit_bytes=VMEM_LIMIT),
        cost_estimate=pl.CostEstimate(flops=75 * fields.size, bytes_accessed=12 * fields.size, transcendentals=0),
        name="inner",
    )(fields, depth, levels)


def ends_kernel(inner_ref, strip_ref, before_ref, after_ref, out_ref, result_ref, sems, *scratch):
    lane = lanes_of(LAT)
    place = (lane + (WIDTH - ring_base(0))) % TILE
    in_after = (place >= STRIP) & (place < STRIP + HALO)
    in_before = (place >= STRIP + HALO) & (place < 2 * STRIP)
    before = before_ref[...]
    after = after_ref[...]
    for kind in range(FIELDS + 1):
        for which in range(2):
            slot = kind * 2 + which
            low = HALO * slot
            values = jnp.where(
                in_after,
                turned(after, ring_base(0) + STRIP - low - HALO),
                jnp.where(
                    in_before, turned(before, ring_base(0) + STRIP + HALO - low), strip_ref[slot]
                ),
            )
            scratch[kind][which, PAD : PAD + LAT, :] = values

    copies = []

    def emit(kind, which, values):
        for half in range(2):
            base = ring_base(half)
            at = kind * LEV + PAIRS[which][half]
            last_columns = turned(values, WIDTH - STRIP - base)
            first_columns = turned(values, -(base + 2 * STRIP))
            result_ref[at] = jnp.where(
                lane < HALO, first_columns, jnp.where(lane >= WIDTH - HALO, last_columns, inner_ref[at])
            )
            copies.append(pltpu.make_async_copy(result_ref.at[at], out_ref.at[at], sems.at[at]))
            copies[-1].start()

    march(scratch, 2, couple_pairs(), emit)
    for copy in copies:
        copy.wait()


def run_ends(inner, strips, before, after):
    return pl.pallas_call(
        ends_kernel,
        out_shape=jax.ShapeDtypeStruct(inner.shape, inner.dtype),
        in_specs=vmem(4),
        out_specs=pl.BlockSpec(memory_space=pl.ANY),
        scratch_shapes=[pltpu.VMEM(inner.shape, inner.dtype), pltpu.SemaphoreType.DMA((FIELDS * LEV,))] + scratch_for(2),
        compiler_params=pltpu.CompilerParams(vmem_limit_bytes=VMEM_LIMIT),
        cost_estimate=pl.CostEstimate(flops=40 * inner.size, bytes_accessed=12 * inner.size, transcendentals=0),
        name="ends",
    )(inner, strips, before, after)


def run_forecast(fields, depth, levels, before, after):
    inner, strips = run_inner(fields, depth, levels)
    return run_ends(inner, strips, before, after)


def ring(values, axis, shift):
    size = lax.axis_size(axis)
    return lax.ppermute(values, axis, [(i, (i + shift) % size) for i in range(size)])


def take_turns(values):
    bands = lax.axis_size("lon")
    halves, columns, layers = DOM
    pairs = []
    for here in range(halves * columns * layers):
        half, column, layer = here // (columns * layers), here // layers % columns, here % layers
        there = (half + HOP[0]) % halves
        there = there * columns + (column + HOP[1]) % columns
        there = there * layers + (layer + HOP[2]) % layers
        pairs += [(here * bands + band, there * bands + band) for band in range(1, bands, 2)]
    return lax.ppermute(values, ("dom", "lon"), pairs)


def on_device(state, level_thickness, wet_levels, ancestors):
    size = lax.axis_size("dom")
    own = ancestors.reshape(1, -1)
    left = ring(own, "lon", 1)
    right = ring(own, "lon", -1)
    chunks = make_chunks(state.reshape(size, -1, WIDTH))
    left, right = lax.optimization_barrier((left, right))
    chunks = add_table(chunks, own, left, right, take_turns(left), size)
    sent = chunks.reshape(size, -1, 1, WIDTH)
    block = lax.all_to_all(sent, "dom", split_axis=0, concat_axis=0, tiled=True)
    mixed = blend(block.reshape(chunks.shape), size)
    back = lax.all_to_all(mixed, "dom", split_axis=0, concat_axis=0, tiled=True)
    fields = back.reshape(FIELDS * LEV, LAT, WIDTH)
    right, left = pack(fields, level_thickness, wet_levels)
    before = ring(right, "lon", 1)
    after = ring(left, "lon", -1)
    result = run_forecast(fields, level_thickness, wet_levels, before, after)
    return result.reshape(state.shape)


def solution(mesh):
    return jax.shard_map(
        on_device,
        mesh=mesh,
        in_specs=(
            P("dom", None, None, None, "lon"),
            P(None, None, "lon"),
            P(None, "lon"),
            P("dom", "lon", None),
        ),
        out_specs=P("dom", None, None, None, "lon"),
        check_vma=False,
    )
```

```python
import jax
import jax.numpy as jnp
from jax import lax
from jax.experimental import pallas as pl
from jax.experimental.pallas import tpu as pltpu
from jax.sharding import PartitionSpec as P

LEV = 4
FIELDS = 4
TILE = 64
BLEND = 8
STEPS = 3
LAT = 128
WIDTH = 128
HALO = 2 * STEPS
PAIRS = ((0, 3), (1, 2))
DOM = (2, 4, 8)
HOP = (1, 2, 4)
PAD = 8

time_step = 0.3
gravity = 1.0
drag_rate = 0.05
diffusion = 0.1
vertical_mix = 0.2
coriolis_base = 0.1
coriolis_slope = 0.3

VMEM_LIMIT = 16 * 1024 * 1024


def lanes_of(rows):
    return lax.broadcasted_iota(jnp.int32, (rows, WIDTH), 1)


def vmem(count):
    return [pl.BlockSpec(memory_space=pltpu.VMEM)] * count


def chunk_kernel(state_ref, out_ref):
    height = state_ref.shape[1]
    for chunk in range(state_ref.shape[0]):
        base = chunk * (height + 1)
        out_ref[base : base + height, :] = state_ref[chunk]


def make_chunks(chunks):
    count, height, width = chunks.shape
    shape = (count * (height + 1), width)
    return pl.pallas_call(
        chunk_kernel,
        out_shape=jax.ShapeDtypeStruct(shape, chunks.dtype),
        in_specs=vmem(1),
        out_specs=pl.BlockSpec(memory_space=pltpu.VMEM),
        compiler_params=pltpu.CompilerParams(vmem_limit_bytes=VMEM_LIMIT),
        cost_estimate=pl.CostEstimate(flops=0, bytes_accessed=8 * chunks.size, transcendentals=0),
        name="chunks",
    )(chunks)


def add_table(chunks, own, left, right, turn, count):
    height = chunks.shape[0] // count

    def table_kernel(turn_ref, own_ref, left_ref, right_ref, chunks_ref, out_ref):
        del turn_ref, chunks_ref
        tile = lanes_of(1) % 4
        picks = (left_ref[0:1, 1:2], own_ref[0:1, 0:1], own_ref[0:1, 1:2], right_ref[0:1, 0:1])
        row = jnp.zeros((1, WIDTH), jnp.int32)
        for at, pick in enumerate(picks):
            row = jnp.where(tile == at, pick, row)
        row = row.astype(jnp.float32)
        for chunk in range(count):
            base = chunk * height + height - 1
            out_ref[base : base + 1, :] = row

    return pl.pallas_call(
        table_kernel,
        out_shape=jax.ShapeDtypeStruct(chunks.shape, chunks.dtype),
        in_specs=vmem(5),
        out_specs=pl.BlockSpec(memory_space=pltpu.VMEM),
        input_output_aliases={4: 0},
        compiler_params=pltpu.CompilerParams(vmem_limit_bytes=VMEM_LIMIT),
        cost_estimate=pl.CostEstimate(flops=0, bytes_accessed=4 * count * WIDTH, transcendentals=0),
        name="table",
    )(turn, own, left, right, chunks)


SHARE = WIDTH // 4
TOGETHER = 8
BROWS = 32
UNROLL = 8


def blend_kernel(block_ref, out_ref, numbers_ref, table_ref, sem):
    particles, rows, _ = out_ref.shape
    table = block_ref[pl.ds(rows, particles, stride=rows + 1), :]
    holder = lax.broadcasted_iota(jnp.int32, (particles, WIDTH), 0) % SHARE
    table = jnp.where(lanes_of(particles) // 4 == holder, table, 0.0)
    for line in range(particles // SHARE):
        total = jnp.sum(table[line * SHARE : (line + 1) * SHARE], axis=0, keepdims=True)
        numbers_ref[line : line + 1, :] = total.astype(jnp.int32)
    copy = pltpu.make_async_copy(numbers_ref, table_ref, sem)
    copy.start()
    lane = lanes_of(BROWS)
    position = lane % TILE
    near_left = position < BLEND
    near_right = position >= TILE - BLEND
    distance = jnp.where(near_left, position, TILE - 1 - position).astype(jnp.float32)
    weight = jnp.where(near_left | near_right, 0.5 + (distance + 0.5) / (2.0 * BLEND), 1.0)
    rest = 1.0 - weight
    first = lane < TILE
    zero = jnp.zeros_like(weight)
    weights = (
        jnp.where(first & near_left, rest, zero),
        jnp.where(first, weight, jnp.where(near_left, rest, zero)),
        jnp.where(first, jnp.where(near_right, rest, zero), weight),
        jnp.where(first, zero, jnp.where(near_right, rest, zero)),
    )
    copy.wait()

    def some(at, carry):
        done = []
        for particle in range(TOGETHER):
            particle = at * TOGETHER + particle
            line, first_tile = particle // SHARE, 4 * (particle % SHARE)
            picks = [table_ref[line, first_tile + tile] * (rows + 1) for tile in range(4)]
            for row in range(0, rows, BROWS):
                parts = [block_ref[pl.ds(pick + row, BROWS), :] * w for pick, w in zip(picks, weights)]
                done.append((particle, row, (parts[1] + parts[2]) + (parts[0] + parts[3])))
        for particle, row, values in done:
            out_ref[particle, row : row + BROWS, :] = values
        return carry

    lax.fori_loop(0, particles // TOGETHER, some, 0, unroll=UNROLL)


def blend(block, particles):
    rows = block.shape[0] // particles - 1
    shape = (particles, rows, WIDTH)
    return pl.pallas_call(
        blend_kernel,
        out_shape=jax.ShapeDtypeStruct(shape, block.dtype),
        in_specs=vmem(1),
        out_specs=pl.BlockSpec(memory_space=pltpu.VMEM),
        scratch_shapes=[
            pltpu.VMEM((particles // SHARE, WIDTH), jnp.int32),
            pltpu.SMEM((particles // SHARE, WIDTH), jnp.int32),
            pltpu.SemaphoreType.DMA,
        ],
        compiler_params=pltpu.CompilerParams(vmem_limit_bytes=VMEM_LIMIT),
        cost_estimate=pl.CostEstimate(flops=4 * block.size, bytes_accessed=8 * block.size, transcendentals=0),
        name="blend",
    )(block)


def masked_thickness(depth_ref, levels_ref, level, start, rows):
    wet = levels_ref[pl.ds(start, rows), :] > level
    return jnp.where(wet, depth_ref[level, pl.ds(start, rows), :], 0.0)


def groups():
    for kind in range(FIELDS + 1):
        for which, pair in enumerate(PAIRS):
            for half, level in enumerate(pair):
                yield kind, level, kind * 2 + which, half


def values_of(fields_ref, depth_ref, levels_ref, kind, level, start, rows):
    if kind < FIELDS:
        return fields_ref[kind * LEV + level, pl.ds(start, rows), :]
    return masked_thickness(depth_ref, levels_ref, level, start, rows)


def pack_kernel(fields_ref, depth_ref, levels_ref, right_ref, left_ref):
    lane = lanes_of(PROWS)

    def within(low):
        return ((lane + (WIDTH - low)) % WIDTH) < HALO

    for start in range(0, LAT, PROWS):
        right = jnp.zeros((PROWS, WIDTH), jnp.float32)
        left = jnp.zeros((PROWS, WIDTH), jnp.float32)
        for kind, level, slot, half in groups():
            values = values_of(fields_ref, depth_ref, levels_ref, kind, level, start, PROWS)
            low = half * TILE + HALO * slot
            turned = pltpu.roll(values, (low + HALO) % WIDTH, 1)
            right = jnp.where(within(low), turned, right)
            left = jnp.where(within(low + HALO), turned, left)
        right_ref[start : start + PROWS, :] = right
        left_ref[start : start + PROWS, :] = left


def pack(fields, depth, levels):
    shape = jax.ShapeDtypeStruct((LAT, WIDTH), jnp.float32)
    return pl.pallas_call(
        pack_kernel,
        out_shape=(shape, shape),
        in_specs=vmem(3),
        out_specs=tuple(vmem(2)),
        compiler_params=pltpu.CompilerParams(vmem_limit_bytes=VMEM_LIMIT),
        cost_estimate=pl.CostEstimate(flops=4 * fields.size, bytes_accessed=5 * fields.size, transcendentals=0),
        name="pack",
    )(fields, depth, levels)


def march(scratch, count, couple, emit):
    height, zonal, merid, tracer, thick, flux, south, north = scratch

    def rows_at(ref, shift):
        return ref[:, PAD + shift : PAD + LAT + shift, :]

    def put(ref, values):
        ref[:, PAD : PAD + LAT, :] = values

    def east(values):
        return pltpu.roll(values, WIDTH - 1, 2)

    def west(values):
        return pltpu.roll(values, 1, 2)

    edge = jnp.zeros((count, PAD, WIDTH), jnp.float32)
    for ref in (height, flux, south, north):
        ref[:, 0:PAD, :] = edge
        ref[:, PAD + LAT : 2 * PAD + LAT, :] = edge

    half = 0.5 * time_step
    keep = 1.0 - time_step * drag_rate
    row = lax.broadcasted_iota(jnp.int32, (LAT, WIDTH), 0)
    turn = time_step * (coriolis_base + coriolis_slope * row.astype(jnp.float32) / LAT)
    turn = turn[None]

    for step in range(STEPS):
        last = step == STEPS - 1
        h, u, v, c, t = (rows_at(ref, 0) for ref in (height, zonal, merid, tracer, thick))
        wet = t > 0.0
        dx = east(h) - west(h)
        dy = rows_at(height, 1) - rows_at(height, -1)
        new_u = jnp.where(wet, keep * u + turn * v - (half * gravity) * dx, 0.0)
        new_v = jnp.where(wet, keep * v - turn * u - (half * gravity) * dy, 0.0)
        some, more = diffusion * c, half * c
        along, cross = more * new_u, more * new_v
        across = t * new_u
        put(flux, t * new_v)
        put(south, some - cross)
        put(north, some + cross)
        if last:
            for which in range(count):
                emit(1, which, new_u[which])
                emit(2, which, new_v[which])
        else:
            put(zonal, new_u)
            put(merid, new_v)
        part = h - half * (east(across) - west(across))
        c_part = (1.0 - 4.0 * diffusion) * c + (east(some - along) + west(some + along))
        dy = rows_at(flux, 1) - rows_at(flux, -1)
        new_h = jnp.where(wet, part - half * dy, 0.0)
        new_c = jnp.where(wet, c_part + (rows_at(south, 1) + rows_at(north, -1)), 0.0)
        if last:
            for which in range(count):
                emit(0, which, new_h[which])
        moved = [new_c[which] for which in range(count)]
        wets = [wet[which] for which in range(count)]
        coupled = couple(moved, wets)
        for which in range(count):
            if last:
                emit(3, which, coupled[which])
            else:
                height[which, PAD : PAD + LAT, :] = new_h[which]
                tracer[which, PAD : PAD + LAT, :] = coupled[which]


def exchange(upper, lower, both_wet):
    return jnp.where(both_wet, vertical_mix * (lower - upper), 0.0)


def couple_levels(moved, wets):
    swaps = [exchange(moved[k], moved[k + 1], wets[k] & wets[k + 1]) for k in range(LEV - 1)]
    return [
        moved[0] + swaps[0],
        moved[1] + swaps[1] - swaps[0],
        moved[2] + swaps[2] - swaps[1],
        moved[3] - swaps[2],
    ]


def couple_pairs():
    known = []

    def couple(moved, wets):
        outer, middle = moved
        if not known:
            turned_wet = pltpu.roll(jnp.where(wets[1], 1.0, 0.0), TILE, 1) > 0.0
            known.append(jnp.where(wets[1] & turned_wet, vertical_mix, 0.0))
        across = exchange(outer, middle, wets[0] & wets[1])
        between = known[0] * (pltpu.roll(middle, TILE, 1) - middle)
        return [outer + across, middle + between - across]

    return couple


def scratch_for(count):
    return [pltpu.VMEM((count, LAT + 2 * PAD, WIDTH), jnp.float32)] * 8


STRIP = 2 * HALO
PROWS = 128


def ring_base(half):
    return (WIDTH - STRIP + TILE * half) % WIDTH


def turned(values, shift):
    return pltpu.roll(values, shift % WIDTH, 1) if shift % WIDTH else values


def inner_kernel(fields_ref, depth_ref, levels_ref, out_ref, strip_ref, *scratch):
    lane = lanes_of(LAT)
    place = (lane + (WIDTH - ring_base(0))) % TILE
    second = (lane >= ring_base(1)) & (lane < ring_base(0))
    for kind, level, slot, half in groups():
        values = values_of(fields_ref, depth_ref, levels_ref, kind, level, 0, LAT)
        scratch[kind][level, PAD : PAD + LAT, :] = values
        base = ring_base(half)
        ends = jnp.where(
            place < 2 * STRIP, turned(values, base - (WIDTH - STRIP)), turned(values, base + 2 * STRIP)
        )
        if half:
            strip_ref[slot] = jnp.where(second, ends, strip_ref[slot])
        else:
            strip_ref[slot] = ends

    def emit(kind, level, values):
        out_ref[kind * LEV + level] = values

    march(scratch, LEV, couple_levels, emit)


def run_inner(fields, depth, levels):
    return pl.pallas_call(
        inner_kernel,
        out_shape=(
            jax.ShapeDtypeStruct(fields.shape, fields.dtype),
            jax.ShapeDtypeStruct((2 * (FIELDS + 1), LAT, WIDTH), fields.dtype),
        ),
        in_specs=vmem(3),
        out_specs=tuple(vmem(2)),
        scratch_shapes=scratch_for(LEV),
        compiler_params=pltpu.CompilerParams(vmem_limit_bytes=VMEM_LIMIT),
        cost_estimate=pl.CostEstimate(flops=75 * fields.size, bytes_accessed=12 * fields.size, transcendentals=0),
        name="inner",
    )(fields, depth, levels)


def ends_kernel(inner_ref, strip_ref, before_ref, after_ref, out_ref, result_ref, sems, *scratch):
    lane = lanes_of(LAT)
    place = (lane + (WIDTH - ring_base(0))) % TILE
    in_after = (place >= STRIP) & (place < STRIP + HALO)
    in_before = (place >= STRIP + HALO) & (place < 2 * STRIP)
    before = before_ref[...]
    after = after_ref[...]
    for kind in range(FIELDS + 1):
        for which in range(2):
            slot = kind * 2 + which
            low = HALO * slot
            values = jnp.where(
                in_after,
                turned(after, ring_base(0) + STRIP - low - HALO),
                jnp.where(
                    in_before, turned(before, ring_base(0) + STRIP + HALO - low), strip_ref[slot]
                ),
            )
            scratch[kind][which, PAD : PAD + LAT, :] = values

    copies = []

    def emit(kind, which, values):
        for half in range(2):
            base = ring_base(half)
            at = kind * LEV + PAIRS[which][half]
            last_columns = turned(values, WIDTH - STRIP - base)
            first_columns = turned(values, -(base + 2 * STRIP))
            result_ref[at] = jnp.where(
                lane < HALO, first_columns, jnp.where(lane >= WIDTH - HALO, last_columns, inner_ref[at])
            )
            copies.append(pltpu.make_async_copy(result_ref.at[at], out_ref.at[at], sems.at[at]))
            copies[-1].start()

    march(scratch, 2, couple_pairs(), emit)
    for copy in copies:
        copy.wait()


def run_ends(inner, strips, before, after):
    return pl.pallas_call(
        ends_kernel,
        out_shape=jax.ShapeDtypeStruct(inner.shape, inner.dtype),
        in_specs=vmem(4),
        out_specs=pl.BlockSpec(memory_space=pl.ANY),
        scratch_shapes=[pltpu.VMEM(inner.shape, inner.dtype), pltpu.SemaphoreType.DMA((FIELDS * LEV,))] + scratch_for(2),
        compiler_params=pltpu.CompilerParams(vmem_limit_bytes=VMEM_LIMIT),
        cost_estimate=pl.CostEstimate(flops=40 * inner.size, bytes_accessed=12 * inner.size, transcendentals=0),
        name="ends",
    )(inner, strips, before, after)


def run_forecast(fields, depth, levels, before, after):
    inner, strips = run_inner(fields, depth, levels)
    return run_ends(inner, strips, before, after)


def ring(values, axis, shift):
    size = lax.axis_size(axis)
    return lax.ppermute(values, axis, [(i, (i + shift) % size) for i in range(size)])


def take_turns(values):
    bands = lax.axis_size("lon")
    halves, columns, layers = DOM
    pairs = []
    for here in range(halves * columns * layers):
        half, column, layer = here // (columns * layers), here // layers % columns, here % layers
        there = (half + HOP[0]) % halves
        there = there * columns + (column + HOP[1]) % columns
        there = there * layers + (layer + HOP[2]) % layers
        pairs += [(here * bands + band, there * bands + band) for band in range(1, bands, 2)]
    values = lax.ppermute(values, ("dom", "lon"), pairs)
    return lax.ppermute(values, "lon", [(1, 3), (3, 1)])


def on_device(state, level_thickness, wet_levels, ancestors):
    size = lax.axis_size("dom")
    own = ancestors.reshape(1, -1)
    turn = take_turns(own)
    left = ring(own, "lon", 1)
    right = ring(own, "lon", -1)
    chunks = make_chunks(state.reshape(size, -1, WIDTH))
    chunks = add_table(chunks, own, left, right, turn, size)
    sent = chunks.reshape(size, -1, 1, WIDTH)
    block = lax.all_to_all(sent, "dom", split_axis=0, concat_axis=0, tiled=True)
    mixed = blend(block.reshape(chunks.shape), size)
    back = lax.all_to_all(mixed, "dom", split_axis=0, concat_axis=0, tiled=True)
    fields = back.reshape(FIELDS * LEV, LAT, WIDTH)
    right, left = pack(fields, level_thickness, wet_levels)
    before = ring(right, "lon", 1)
    after = ring(left, "lon", -1)
    result = run_forecast(fields, level_thickness, wet_levels, before, after)
    return result.reshape(state.shape)


def solution(mesh):
    return jax.shard_map(
        on_device,
        mesh=mesh,
        in_specs=(
            P("dom", None, None, None, "lon"),
            P(None, None, "lon"),
            P(None, "lon"),
            P("dom", "lon", None),
        ),
        out_specs=P("dom", None, None, None, "lon"),
        check_vma=False,
    )
```
